32 devices in a mesh: slab: 16 (over z, y, x), sub: 2 (over core).
Axes of the slice: x: 2, y: 2, z: 4, core: 2. Of those that a mesh axis runs over, the one named last changes fastest.
Arguments:
- part_cells: int32 [32, 32, 1024], P(('slab', 'sub')), may hold values from 0 to 8191
- part_offsets: float32 [32, 32, 3, 1024], P(('slab', 'sub')), may hold values from 0 to 1
- part_counts: int32 [32, 32], P(('slab', 'sub')), may hold values from 128 to 1024, as said below
- w_first: bfloat16 [16, 27], replicated, may hold values from -1.25 to 1.25
- w_mid: bfloat16 [16, 432], replicated, may hold values from -0.3125 to 0.3125
- w_last: bfloat16 [16, 432], replicated, may hold values from -0.3125 to 0.3125
- w_head: bfloat16 [3, 32], replicated, may hold values from -1 to 1
- cotangent: bfloat16 [3, 64, 16, 256], P(None, 'slab', 'sub'), may hold values from -6 to 6
Outputs:
- force: bfloat16 [3, 64, 16, 256], P(None, 'slab', 'sub')
- grad_first: float32 [16, 27], replicated
- grad_mid: float32 [16, 432], replicated
- grad_last: float32 [16, 432], replicated
- grad_head: float32 [3, 32], replicated
The draws below stay inside these ranges and needn't reach their ends.
Inputs may be any that keep to these rules, and one draw needn't show every extreme that they name: part_counts[s, d] is the number of used slots among the 1024 slots from device s to brick d; one brick, drawn from the seed, gets 1024 from every device. part_cells[s, d, k] is the cell (i * 8 + j) * 256 + l in brick d's own cells; slots at or above part_counts[s, d] are unused.
All inputs are finite; a program needn't handle non-finite values.
Results may differ from the reference program's by a relative error of at most 0.003.
The reference program's roundings to bfloat16 on the way (of `density_b`, `hidden_one`, `hidden_two`, `hidden_three`, `features`, `grad_three`, `grad_two` and `grad_one`) count: a program that leaves them out, or rounds other values in their place, can miss the bound.
Values may be sent and summed in bfloat16 or wider, within the bound.
No kernel may reach another device: no remote copies, remote signals or barrier semaphores. Data moves between devices by JAX's collectives and lax.ppermute only.
A program may use at most 192 MiB of HBM per device.

```python
import math
import jax
import jax.numpy as jnp
from jax import lax

CH = 16
BX = 4
BY = 8
NZ = 256
CAP = 1024
NX = 64
NY = 16
NCELLS = 262144
N_SUB = 2
DEVICES = 32


def draw_part_counts(key, part):
    key_full, key_level, key_drop = jax.random.split(key, 3)
    full_brick = jax.random.randint(key_full, (), 0, DEVICES)
    levels = jax.random.randint(key_level, (DEVICES,), CAP // 4, CAP + 1)
    drops = jax.random.randint(key_drop, (DEVICES, DEVICES), 0, levels[None, :] // 2 + 1)
    counts = levels[None, :] - drops
    column = jnp.arange(DEVICES) == full_brick
    return jnp.where(column[None, :], CAP, counts).astype(jnp.int32)


def place_ends(array, own_key, low, largest):
    spot = [jax.random.randint(jax.random.fold_in(own_key, axis), (), 0, length) for axis, length in enumerate(array.shape)]
    widest = array.shape.index(max(array.shape))
    next_to = spot[:widest] + [(spot[widest] + 1) % array.shape[widest]] + spot[widest + 1:]
    return array.at[tuple(spot)].set(low).at[tuple(next_to)].set(largest)


def block_scale(own_key, dims, shards, least, high):
    gain, own = 1.0, jax.random.fold_in(own_key, 6)
    for axis_at, blocks in shards:
        draws = jnp.exp(jax.random.uniform(jax.random.fold_in(own, axis_at), (blocks,), jnp.float32, least / len(shards), high / len(shards)))
        gain = gain * jnp.repeat(draws, dims[axis_at] // blocks).reshape([-1 if axis == axis_at else 1 for axis in range(len(dims))])
    return gain


def gaussian(own_key, extent, deviation, limit, cuts=(), kind=jnp.bfloat16):
    level = block_scale(own_key, extent, cuts, -0.22, 0.18) if cuts else 1.0
    values = jax.random.normal(own_key, extent, jnp.float32) * deviation * level
    return jnp.minimum(jnp.maximum(values, -limit), limit).astype(kind)


def setup_inputs(seed: int = 0) -> dict:
    streams_of = jax.random.split(jax.random.key(seed), 9)
    return {
        "part_cells": place_ends(jax.random.randint(streams_of[0], (DEVICES, DEVICES, CAP), 0, BX * BY * NZ), jax.random.fold_in(streams_of[0], 1), 0, (BX * BY * NZ) - 1).astype(jnp.int32),
        "part_offsets": jnp.clip(1.0 * jax.random.uniform(streams_of[1], (DEVICES, DEVICES, 3, CAP), jnp.float32) ** block_scale(streams_of[1], (DEVICES, DEVICES, 3, CAP), ((0, 32),), -0.2, 0.2), 0.0, 1.0),
        "part_counts": draw_part_counts(jax.random.fold_in(streams_of[8], 71), 0),
        "w_first": gaussian(streams_of[3], (CH, 27), 27 ** -0.5, 1.25),
        "w_mid": gaussian(streams_of[4], (CH, 27 * CH), (27 * CH) ** -0.5, 0.3125),
        "w_last": gaussian(streams_of[5], (CH, 27 * CH), (27 * CH) ** -0.5, 0.3125),
        "w_head": gaussian(streams_of[6], (3, 2 * CH), (2 * CH) ** -0.5, 1.0),
        "cotangent": gaussian(streams_of[7], (3, NX, NY, NZ), 1.0, 6.0, ((1, 16), (2, 2))),
    }


def wrap_field(field):
    return jnp.pad(field, ((0, 0), (1, 1), (1, 1), (1, 1)), mode='wrap')

def kernel_of(weights, chans):
    out_chans = weights.shape[0]
    return weights.astype(jnp.float32).reshape(out_chans, 3, 3, 3, chans).transpose(0, 4, 1, 2, 3)

def convolve(field, weights):
    chans = field.shape[0]
    padded = wrap_field(field.astype(jnp.float32))
    result = lax.conv_general_dilated(padded[None], kernel_of(weights, chans), (1, 1, 1), 'VALID', dimension_numbers=('NCDHW', 'OIDHW', 'NCDHW'), precision=lax.Precision.HIGHEST)
    return result[0]

def backward(field, weights, grad):
    _, pullback = jax.vjp(convolve, field.astype(jnp.float32), weights.astype(jnp.float32))
    return pullback(grad.astype(jnp.float32))

def silu_slope(value):
    sigma = jax.nn.sigmoid(value)
    return sigma * (1.0 + value * (1.0 - sigma))

def reference(part_cells, part_offsets, part_counts, w_first, w_mid, w_last, w_head, cotangent):
    slot_ids = jnp.arange(CAP, dtype=jnp.int32)
    live = (slot_ids[None, None, :] < part_counts[:, :, None]).astype(jnp.float32)
    bricks = jnp.arange(DEVICES, dtype=jnp.int32)
    base_x = (bricks // N_SUB * BX)[None, :, None]
    base_y = (bricks % N_SUB * BY)[None, :, None]
    cell_x = base_x + part_cells // (BY * NZ)
    cell_y = base_y + part_cells // NZ % BY
    cell_z = part_cells % NZ
    frac_x = part_offsets[:, :, 0, :]
    frac_y = part_offsets[:, :, 1, :]
    frac_z = part_offsets[:, :, 2, :]
    density = jnp.zeros((NX * NY * NZ,), jnp.float32)
    for corner_x in (0, 1):
        weight_x = frac_x if corner_x else 1.0 - frac_x
        for corner_y in (0, 1):
            weight_y = frac_y if corner_y else 1.0 - frac_y
            for corner_z in (0, 1):
                weight_z = frac_z if corner_z else 1.0 - frac_z
                share = live * weight_x * weight_y * weight_z
                index = ((cell_x + corner_x) % NX * NY + (cell_y + corner_y) % NY) * NZ + (cell_z + corner_z) % NZ
                density = density.at[index.reshape(-1)].add(share.reshape(-1))
    density_b = density.reshape(1, NX, NY, NZ).astype(jnp.bfloat16)
    pre_one = convolve(density_b, w_first)
    hidden_one = jax.nn.silu(pre_one).astype(jnp.bfloat16)
    pre_two = convolve(hidden_one, w_mid)
    hidden_two = jax.nn.silu(pre_two).astype(jnp.bfloat16)
    pre_three = convolve(hidden_two, w_last)
    hidden_three = jax.nn.silu(pre_three).astype(jnp.bfloat16)
    features = jnp.concatenate([hidden_three, hidden_one], 0).reshape(2 * CH, -1)
    ct_flat = cotangent.reshape(3, -1)
    force = jnp.dot(w_head, features, preferred_element_type=jnp.float32).astype(jnp.bfloat16).reshape(3, NX, NY, NZ)
    loss_scale = 1.0 / math.sqrt(NCELLS)
    grad_head = loss_scale * jnp.dot(ct_flat, features.T, preferred_element_type=jnp.float32)
    back_features = jnp.dot(w_head.T, ct_flat, preferred_element_type=jnp.float32)
    grad_three = (back_features[:CH] * silu_slope(pre_three.reshape(CH, -1))).astype(jnp.bfloat16).reshape(CH, NX, NY, NZ)
    back_two, grad_last = backward(hidden_two, w_last, grad_three)
    grad_two = (back_two * silu_slope(pre_two)).astype(jnp.bfloat16)
    back_one, grad_mid = backward(hidden_one, w_mid, grad_two)
    back_one = back_one + back_features[CH:].reshape(CH, NX, NY, NZ)
    grad_one = (back_one * silu_slope(pre_one)).astype(jnp.bfloat16)
    _, grad_first = backward(density_b, w_first, grad_one)
    return (force, loss_scale * grad_first, loss_scale * grad_mid, loss_scale * grad_last, grad_head)
```

```python
import functools
import math

import jax
import jax.numpy as jnp
from jax import lax
from jax.experimental import pallas as pl
from jax.experimental.pallas import tpu as pltpu
from jax.sharding import PartitionSpec as P

BITS = 21
STEPS = 1 << BITS


def pack_kernel(dead, cells_hbm, offsets_hbm, counts_hbm, words_ref, cells_ref, offsets_ref, counts_ref, sems):
    dests, cap = cells_ref.shape
    copies = [
        pltpu.make_async_copy(source, target, sems.at[i])
        for i, (source, target) in enumerate(
            ((counts_hbm, counts_ref), (cells_hbm, cells_ref), (offsets_hbm, offsets_ref))
        )
    ]
    for copy in copies:
        copy.start()
    for copy in copies:
        copy.wait()
    eye = lax.broadcasted_iota(jnp.int32, (dests, dests), 0) == lax.broadcasted_iota(jnp.int32, (dests, dests), 1)
    counts = jnp.where(eye, counts_ref[...].astype(jnp.float32), 0.0)
    counts = jnp.sum(counts, axis=1, keepdims=True).astype(jnp.int32)
    live = lax.broadcasted_iota(jnp.int32, (dests, cap), 1) < counts
    code = jnp.where(live, cells_ref[...], dead)
    fixed = [
        jnp.minimum((offsets_ref[i] * STEPS + 0.5).astype(jnp.int32), STEPS - 1) for i in range(3)
    ]
    first = fixed[0] | (fixed[2] << BITS)
    second = fixed[1] | ((fixed[2] >> (32 - BITS)) << BITS)
    codes = code[:, : cap // 2] | (code[:, cap // 2 :] << 16)
    for dest in range(dests):
        words_ref[dest, :, 0:cap] = first[dest : dest + 1]
        words_ref[dest, :, cap : 2 * cap] = second[dest : dest + 1]
        words_ref[dest, :, 2 * cap :] = codes[dest : dest + 1]


def packed_slots(cells, offsets, counts, width_x, width_y, depth_z):
    dests, cap = cells.shape
    return pl.pallas_call(
        functools.partial(pack_kernel, 2 * width_x * width_y * depth_z),
        out_shape=jax.ShapeDtypeStruct((dests, 1, 5 * cap // 2), jnp.int32),
        in_specs=[pl.BlockSpec(memory_space=pltpu.HBM)] * 3,
        out_specs=pl.BlockSpec(memory_space=pltpu.VMEM),
        scratch_shapes=[
            pltpu.VMEM((dests, cap), jnp.int32),
            pltpu.VMEM((3, dests, cap), jnp.float32),
            pltpu.VMEM((1, dests), jnp.int32),
            pltpu.SemaphoreType.DMA((3,)),
        ],
        compiler_params=pltpu.CompilerParams(vmem_limit_bytes=60 * 1024 * 1024),
        name="pack",
    )(cells, offsets.transpose(1, 0, 2), counts)


def deposit_kernel(width_x, width_y, depth_z, cap, words_ref, after_ref, late_ref, out_ref, acc_ref):
    rows = out_ref.shape[0]
    acc_ref[...] = jnp.zeros_like(acc_ref)
    slot_rows = cap // 128
    source_rows = slot_rows * 5 // 2
    group = 16 // slot_rows
    row_id = lax.broadcasted_iota(jnp.int32, (8, 128), 0)
    z_id = lax.broadcasted_iota(jnp.int32, (depth_z, 128), 0).astype(jnp.float32).astype(jnp.bfloat16)
    one, zero = jnp.bfloat16(1.0), jnp.bfloat16(0.0)

    def body(i, carry):
        block = words_ref[pl.ds(pl.multiple_of(i * group * source_rows, 8), group * source_rows), :]

        def gathered(start, length):
            parts = [block[k * source_rows + start : k * source_rows + start + length] for k in range(group)]
            return parts

        first = jnp.concatenate(gathered(0, slot_rows), axis=0)
        second = jnp.concatenate(gathered(slot_rows, slot_rows), axis=0)
        halves = gathered(2 * slot_rows, slot_rows // 2)
        code = jnp.concatenate([part for half in halves for part in (half & 0xFFFF, (half >> 16) & 0xFFFF)], axis=0)
        inv = 1.0 / STEPS
        fixed_z = ((first >> BITS) & ((1 << (32 - BITS)) - 1)) | ((second >> BITS) << (32 - BITS))
        frac_x = (first & (STEPS - 1)).astype(jnp.float32) * inv
        frac_y = (second & (STEPS - 1)).astype(jnp.float32) * inv
        frac_z = fixed_z.astype(jnp.float32) * inv
        cell_z = (code % depth_z).astype(jnp.float32)
        column = code // depth_z
        cell_y = column % width_y
        cell_x = column // width_y
        past = jnp.where(cell_y == width_y - 1, frac_y, 0.0)
        rest_x, rest_y, rest_z = 1.0 - frac_x, 1.0 - frac_y, 1.0 - frac_z
        weights, hot = [], []
        for k in range(16):
            row = slice(k, k + 1)
            at_y, at_x = cell_y[row], cell_x[row]
            wy = jnp.where(at_y == row_id, rest_y[row], jnp.where(at_y + 1 == row_id, frac_y[row], 0.0))
            wx = jnp.where(at_x == row_id, rest_x[row], jnp.where(at_x + 1 == row_id, frac_x[row], 0.0))
            parts = [wx[x : x + 1] * wy for x in range(width_x + 1)] + [wx * past[row]]
            area = jnp.concatenate(parts, axis=0)
            low, high = area * rest_z[row], area * frac_z[row]
            low_a, high_a = low.astype(jnp.bfloat16), high.astype(jnp.bfloat16)
            low_b = (low - low_a.astype(jnp.float32)).astype(jnp.bfloat16)
            high_b = (high - high_a.astype(jnp.float32)).astype(jnp.bfloat16)
            weights.append(jnp.concatenate([low_a, low_b, high_a, high_b], axis=0))
            at_z = jnp.broadcast_to(cell_z[row], (depth_z, 128)).astype(jnp.bfloat16)
            hot.append(jnp.where(at_z == z_id, one, zero))
        acc_ref[...] += lax.dot_general(
            jnp.concatenate(weights, axis=1),
            jnp.concatenate(hot, axis=1),
            (((1,), (1,)), ((), ())),
            preferred_element_type=jnp.float32,
        )
        return carry

    lax.fori_loop(0, words_ref.shape[0] // (group * source_rows), body, 0, unroll=8)
    low = acc_ref[0:rows] + acc_ref[rows : 2 * rows]
    high = acc_ref[2 * rows : 3 * rows] + acc_ref[3 * rows : 4 * rows]
    out_ref[...] = low + pltpu.roll(high, 1, axis=1)


def deposit(words, after, late, cap, width_x, width_y, depth_z):
    rows = (width_x + 1) * width_y + 8
    return pl.pallas_call(
        functools.partial(deposit_kernel, width_x, width_y, depth_z, cap),
        out_shape=jax.ShapeDtypeStruct((rows, depth_z), jnp.float32),
        in_specs=[pl.BlockSpec(memory_space=pltpu.VMEM)] * 3,
        out_specs=pl.BlockSpec(memory_space=pltpu.VMEM),
        scratch_shapes=[pltpu.VMEM((4 * rows, depth_z), jnp.float32)],
        compiler_params=pltpu.CompilerParams(vmem_limit_bytes=16 * 1024 * 1024),
        name="deposit",
    )(words.reshape(-1, 128), after, late)


def combine_kernel(width_x, width_y, own_ref, other_ref, near_ref, far_ref):
    full_y = 2 * width_y
    spill = (width_x + 1) * width_y
    top = lax.broadcasted_iota(jnp.int32, (width_y, own_ref.shape[1]), 0) == 0
    planes = []
    for x in range(width_x + 1):
        rows, edge = slice(x * width_y, (x + 1) * width_y), slice(spill + x, spill + x + 1)
        upper = own_ref[rows] + jnp.where(top, other_ref[edge], 0.0)
        lower = other_ref[rows] + jnp.where(top, own_ref[edge], 0.0)
        near_ref[x * full_y : x * full_y + width_y] = upper
        near_ref[x * full_y + width_y : (x + 1) * full_y] = lower
        planes.append((upper, lower))
    upward = lax.axis_index("sub") == 0
    for i, (up, down) in enumerate(((width_x - 1, 0), (width_x, 0))):
        for half in range(2):
            start = i * full_y + half * width_y
            far_ref[start : start + width_y] = jnp.where(upward, planes[up][half], planes[down][half])


def combined(own, other, width_x, width_y):
    depth_z = own.shape[1]
    full_y = 2 * width_y
    return pl.pallas_call(
        functools.partial(combine_kernel, width_x, width_y),
        out_shape=(
            jax.ShapeDtypeStruct(((width_x + 1) * full_y, depth_z), jnp.float32),
            jax.ShapeDtypeStruct((2 * full_y, depth_z), jnp.float32),
        ),
        in_specs=[pl.BlockSpec(memory_space=pltpu.VMEM)] * 2,
        out_specs=(pl.BlockSpec(memory_space=pltpu.VMEM),) * 2,
        compiler_params=pltpu.CompilerParams(vmem_limit_bytes=4 * 1024 * 1024),
        name="combine",
    )(own, other)


CH = 16


def dot(a, b, dims=((1,), (0,))):
    return lax.dot_general(a, b, (dims, ((), ())), preferred_element_type=jnp.float32)


def iota(shape, axis):
    return lax.broadcasted_iota(jnp.int32, shape, axis)


def weights_kernel(
    full_y, raw_ref, after_ref, mats_ref, wfirst_ref, whead_ref, square, taps_ref
):
    lanes = full_y * CH
    f32, bf16 = jnp.float32, jnp.bfloat16
    slot = iota((CH, 128), 1) // CH

    def turned(x, by):
        return x if by % 128 == 0 else pltpu.roll(x, by % 128, axis=1)

    square[...] = jnp.zeros_like(square)
    for which in range(2):
        square[0:CH, :] = raw_ref[:, which * 512 : (which + 1) * 512].astype(f32)
        flipped = jnp.transpose(square[...])
        for dx in range(3):
            for dz in range(3):
                ahead = back = jnp.zeros((CH, 128), f32)
                for dy in range(3):
                    start = (dx * 9 + dy * 3 + dz) * CH
                    ahead = ahead + turned(flipped[start : start + CH], dy * CH)
                    block = start // 128 * 128
                    picked = jnp.where(slot == (start - block) // CH, square[0:CH, block : block + 128], 0.0)
                    back = back + turned(picked, dy * CH - (start - block))
                rows = slice((dx * 3 + dz) * CH, (dx * 3 + dz + 1) * CH)
                taps_ref[which, rows, :] = ahead.astype(bf16)
                taps_ref[2 + which, rows, :] = back.astype(bf16)

    row, lane = iota((128, lanes), 0), iota((128, lanes), 1)
    same = row % CH == lane % CH
    shift, lane_y = row // CH - 1, lane // CH

    def body(y, carry):
        forward = jnp.where(same & (lane_y == (y - shift + full_y) % full_y), 1.0, 0.0).astype(bf16)
        back = jnp.where(same & (lane_y == (y + shift + full_y) % full_y), 1.0, 0.0).astype(bf16)
        for which in range(4):
            spread = dot(taps_ref[which], forward if which < 2 else back).astype(bf16)
            for dx in range(3):
                for dz in range(3):
                    tap = dx * 3 + dz if which < 2 else (2 - dx) * 3 + 2 - dz
                    start = pl.multiple_of(dz * lanes + y * CH, CH)
                    mats_ref[which, dx, pl.ds(start, CH), :] = spread[tap * CH : (tap + 1) * CH]
        return carry

    lax.fori_loop(0, full_y, body, 0, unroll=4)

    rows = 9 * full_y
    at_y, at_lane = iota((rows, lanes), 0) % full_y, iota((rows, lanes), 1) // CH
    square[...] = jnp.zeros_like(square)
    square[0:CH, 0:128] = raw_ref[:, 1024:1152].astype(f32)
    flipped = jnp.transpose(square[:, 0:128])
    spread_rows = []
    for dx in range(3):
        for dz in range(3):
            line = jnp.zeros((1, 128), f32)
            for dy in range(3):
                tap = dx * 9 + dy * 3 + dz
                line = line + turned(flipped[tap : tap + 1], dy * CH)
            spread_rows.append(jnp.broadcast_to(line, (full_y, 128)))
    first = jnp.concatenate(spread_rows, axis=0).astype(bf16)
    total = jnp.zeros((rows, lanes), f32)
    for dy in range(3):
        pick = jnp.where(same & (row // CH == dy), 1.0, 0.0).astype(bf16)
        total = jnp.where(at_y == (at_lane + dy - 1 + full_y) % full_y, dot(first, pick), total)
    wfirst_ref[...] = total.astype(bf16)

    rows = 3 * full_y
    at_y, at_lane = iota((rows, lanes), 0) % full_y, iota((rows, lanes), 1) // CH
    square[...] = jnp.zeros_like(square)
    square[0:CH, 0:128] = raw_ref[:, 1152:1280].astype(f32)
    head = [jnp.broadcast_to(square[k : k + 1, 0:128], (full_y, 128)) for k in range(3)]
    head = jnp.concatenate(head, axis=0).astype(bf16)
    for half in range(2):
        pick = jnp.where(row == lane % CH + half * CH, 1.0, 0.0).astype(bf16)
        whead_ref[half] = jnp.where(at_y == at_lane, dot(head, pick), 0.0).astype(bf16)


def side_by_side(w_first, w_mid, w_last, w_head):
    def widened(w, columns):
        return jnp.pad(w, ((0, CH - w.shape[0]), (0, columns - w.shape[1])))

    return jnp.concatenate([widened(w_mid, 512), widened(w_last, 512), widened(w_first, 128), widened(w_head, 128)], axis=1)


def weight_matrices(raw, after, full_y):
    lanes = full_y * CH
    return pl.pallas_call(
        functools.partial(weights_kernel, full_y),
        out_shape=(
            jax.ShapeDtypeStruct((4, 3, 3 * lanes, lanes), jnp.bfloat16),
            jax.ShapeDtypeStruct((9 * full_y, lanes), jnp.bfloat16),
            jax.ShapeDtypeStruct((2, 3 * full_y, lanes), jnp.bfloat16),
        ),
        in_specs=[pl.BlockSpec(memory_space=pltpu.VMEM)] * 2,
        out_specs=(pl.BlockSpec(memory_space=pltpu.VMEM),) * 3,
        scratch_shapes=[pltpu.VMEM((128, 512), jnp.float32), pltpu.VMEM((4, 9 * CH, 128), jnp.bfloat16)],
        compiler_params=pltpu.CompilerParams(vmem_limit_bytes=16 * 1024 * 1024),
        cost_estimate=pl.CostEstimate(flops=2 * 4 * 9 * CH * 128 * lanes * full_y, bytes_accessed=8 << 20, transcendentals=0),
        name="weights",
    )(raw, after)


def edges_kernel(width_x, width_y, own_ref, other_ref, middle_ref, edge_ref):
    full_y = 2 * width_y
    upward = lax.axis_index("sub") == 0
    for k in range(3):
        rows = slice(k * full_y, (k + 1) * full_y)
        planes = []
        for x in range(width_x):
            both = [own_ref[k, x].astype(jnp.float32), other_ref[k, x].astype(jnp.float32)]
            planes.append(jnp.concatenate(both, axis=0))
            middle_ref[x, rows] = planes[x].astype(jnp.bfloat16)
        for i in range(2):
            edge_ref[i, rows] = jnp.where(upward, planes[width_x - 2 + i], planes[i]).astype(jnp.bfloat16)


def edges(own, other):
    _, width_x, width_y, depth_z = own.shape
    return pl.pallas_call(
        functools.partial(edges_kernel, width_x, width_y),
        out_shape=(
            jax.ShapeDtypeStruct((width_x, 6 * width_y, depth_z), jnp.bfloat16),
            jax.ShapeDtypeStruct((2, 6 * width_y, depth_z), jnp.bfloat16),
        ),
        in_specs=[pl.BlockSpec(memory_space=pltpu.VMEM)] * 2,
        out_specs=(pl.BlockSpec(memory_space=pltpu.VMEM),) * 2,
        compiler_params=pltpu.CompilerParams(vmem_limit_bytes=4 * 1024 * 1024),
        name="edges",
    )(own, other)


def sigmoid(v):
    return 0.5 + 0.5 * jnp.tanh(0.5 * v)


def chain_kernel(
    width_x,
    width_y,
    near_ref,
    near_mine,
    near_theirs,
    far_mine,
    far_theirs,
    ct_middle,
    ct_mine,
    ct_theirs,
    mats_ref,
    wfirst_ref,
    whead_ref,
    force_ref,
    mine_ref,
    ct_ref,
    dens,
    fields,
    three,
    grads,
    pre_one,
    pre_two,
    wg,
):
    full_y = 2 * width_y
    depth = ct_ref.shape[2]
    lanes = full_y * CH
    own = width_y * CH
    first_core = lax.axis_index("sub") == 0

    def turned(ref, plane):
        start = plane * full_y
        return jnp.concatenate([ref[start + width_y : start + full_y], ref[start : start + width_y]], axis=0)

    def straight(ref, plane):
        return ref[plane * full_y : (plane + 1) * full_y]

    planes = [straight(near_ref, x) for x in range(width_x + 1)]
    below = [jnp.where(first_core, straight(near_mine, x), turned(near_theirs, x)) for x in range(width_x + 1)]
    above = [jnp.where(first_core, turned(near_theirs, x), straight(near_mine, x)) for x in range(width_x + 1)]
    tail = [jnp.where(first_core, straight(far_mine, x), turned(far_theirs, x)) for x in range(2)]
    ahead = jnp.where(first_core, turned(far_theirs, 0), straight(far_mine, 0))
    column = [tail[0], tail[1] + below[0], *below[1:width_x], below[width_x] + planes[0], *planes[1:width_x]]
    column = column + [planes[width_x] + above[0], *above[1:width_x], above[width_x] + ahead]
    n_dens = 3 * width_x + 2
    for j in range(n_dens):
        plane = column[j]
        around = [pltpu.roll(plane, 1, axis=1), plane, pltpu.roll(plane, depth - 1, axis=1)]
        dens[3 * full_y * j : 3 * full_y * (j + 1)] = jnp.concatenate(around, axis=0).astype(jnp.bfloat16)

    for x in range(width_x):
        ct_ref[x + 2] = ct_middle[x]
    for x in range(2):
        mine, theirs = ct_mine[x].astype(jnp.float32), ct_theirs[x].astype(jnp.float32)
        halves = [theirs[i * width_y : (i + 1) * width_y] for i in (1, 0, 3, 2, 5, 4)]
        theirs = jnp.concatenate(halves, axis=0)
        ct_ref[x] = jnp.where(first_core, mine, theirs).astype(jnp.bfloat16)
        ct_ref[x + 2 + width_x] = jnp.where(first_core, theirs, mine).astype(jnp.bfloat16)

    def window(x):
        return dens[pl.ds(pl.multiple_of(3 * full_y * x, 3 * full_y), 9 * full_y), :]

    def put(ref, x, field):
        ref[x, :, 0:lanes] = pltpu.roll(field, 1, axis=0).astype(jnp.bfloat16)
        ref[x, :, lanes : 2 * lanes] = field.astype(jnp.bfloat16)
        ref[x, :, 2 * lanes : 3 * lanes] = pltpu.roll(field, depth - 1, axis=0).astype(jnp.bfloat16)

    def conv(ref, x, which, columns=lanes):
        field = jnp.concatenate([ref[x + dx : x + dx + 2].reshape(2 * depth, 3 * lanes) for dx in range(3)], axis=1)
        weights = mats_ref[which].reshape(9 * lanes, lanes)[:, 0:columns]
        return dot(field, weights).reshape(2, depth, columns)

    def slope(v):
        s = sigmoid(v)
        return s * (1.0 + v * (1.0 - s))

    one, two = 0, n_dens - 2
    g_three, g_two = 0, n_dens - 6

    for x in range(n_dens - 2):
        v = dot(window(x), wfirst_ref[...], ((0,), (0,)))
        if 0 <= x - 4 < width_x:
            pre_one[x - 4] = v[:, 0:own]
        put(fields, one + x, v * sigmoid(v))

    for i in range((n_dens - 4) // 2):
        both = conv(fields, one + 2 * i, 0)
        for k in range(2):
            v, x = both[k], 2 * i + k
            if 0 <= x - 2 < width_x + 2:
                pre_two[x - 2] = v
            put(fields, two + x, v * sigmoid(v))

    for i in range((n_dens - 6) // 2):
        both = conv(fields, two + 2 * i, 1)
        for k in range(2):
            v, x = both[k], 2 * i + k
            s = sigmoid(v)
            if 0 <= x - 2 < width_x:
                three[x - 2] = (v * s).astype(jnp.bfloat16)
            back = dot(ct_ref[x], whead_ref[0], ((0,), (0,)))
            put(grads, g_three + x, back * (s * (1.0 + v * (1.0 - s))))

    ct_own = jnp.concatenate([ct_ref[x + 2] for x in range(width_x)], axis=1)
    heads = [
        dot(ct_own, three[:, :, 0:own].reshape(width_x * depth, own)),
        dot(ct_own, fields[one + 4 : one + 4 + width_x, :, lanes : lanes + own].reshape(width_x * depth, own)),
    ]
    for x in range(width_x):
        h_three, h_one = three[x], fields[one + x + 4, :, lanes : 2 * lanes]
        rows = dot(whead_ref[0], h_three, ((1,), (1,))) + dot(whead_ref[1], h_one, ((1,), (1,)))
        for k in range(3):
            force_ref[k, x] = rows[k * full_y : k * full_y + width_y].astype(jnp.bfloat16)

    for i in range((width_x + 2) // 2):
        both = conv(grads, g_three + 2 * i, 3)
        for k in range(2):
            x = 2 * i + k
            put(grads, g_two + x, both[k] * slope(pre_two[x]))

    grad_base = jnp.where(first_core, g_three + 2, g_two + 1)
    field_base = jnp.where(first_core, two + 2, one + 3)
    across = []
    for x in range(width_x):
        grad = grads[grad_base + x, :, lanes : 2 * lanes].astype(jnp.float32)
        across.append(jnp.transpose(grad).astype(jnp.bfloat16))
    across = jnp.concatenate(across, axis=1)
    for dx in range(3):
        field = fields[pl.ds(field_base + dx, width_x)].reshape(width_x * depth, 3 * lanes)
        wg[dx] = dot(across, field)
    grad_one = []
    for i in range(width_x // 2):
        both = conv(grads, g_two + 2 * i, 2, own)
        for k in range(2):
            x = 2 * i + k
            total = both[k] + dot(ct_ref[x + 2], whead_ref[1, :, 0:own], ((0,), (0,)))
            grad_one.append((total * slope(pre_one[x])).astype(jnp.bfloat16))
    windows = jnp.concatenate([window(x + 4) for x in range(width_x)], axis=1)
    firsts = dot(windows, jnp.concatenate(grad_one, axis=0))

    lane = iota((CH, 128), 1)
    blocks = [jnp.zeros((CH, 128), jnp.float32) for _ in range(4)]
    for dx in range(3):
        for dz in range(3):
            lined = jnp.zeros((CH, lanes), jnp.float32)
            for y in range(full_y):
                piece = wg[dx, y * CH : (y + 1) * CH, dz * lanes : (dz + 1) * lanes]
                turn = (lanes - CH * (y - 1)) % lanes
                lined = lined + (piece if turn == 0 else pltpu.roll(piece, turn, axis=1))
            for dy in range(3):
                target = (dx * 9 + dy * 3 + dz) * CH
                turn = (target - dy * CH) % 128
                piece = jnp.where(lane // CH == dy, lined[:, 0:128], 0.0)
                blocks[target // 128] += piece if turn == 0 else pltpu.roll(piece, turn, axis=1)
    def folded(rows):
        for turn in (64, 32, 16):
            rows = rows + pltpu.roll(rows, turn, axis=1)
        return rows

    at_y, at_lane = iota((full_y, own), 0), iota((full_y, own), 1) // CH
    first_rows = []
    for dx in range(3):
        for dy in range(3):
            match = at_y == (at_lane + dy - 1 + full_y) % full_y
            for dz in range(3):
                tap = (dx * 3 + dz) * full_y
                part = jnp.where(match, firsts[tap : tap + full_y, :], 0.0)
                first_rows.append(jnp.sum(part, axis=0, keepdims=True))
    first = folded(jnp.concatenate(first_rows + [jnp.zeros((5, own), jnp.float32)], axis=0))
    gap = jnp.zeros((48, own), jnp.float32)
    blocks[3] += jnp.transpose(jnp.concatenate([gap, first, gap], axis=0))[0:CH]
    for half in range(2):
        rows = []
        for k in range(3):
            part = jnp.where(at_y == at_lane, heads[half][k * full_y : (k + 1) * full_y], 0.0)
            rows.append(jnp.sum(part, axis=0, keepdims=True))
        head = folded(jnp.concatenate(rows + [jnp.zeros((CH - 3, own), jnp.float32)], axis=0))
        blocks[3] += jnp.where(lane // CH == 5 + half, head, 0.0)
    for block in range(4):
        mine_ref[:, block * 128 : (block + 1) * 128] = blocks[block]


def chain(pieces, mats, wfirst, whead, width_x, width_y, depth_z):
    full_y = 2 * width_y
    lanes, own = full_y * CH, width_y * CH
    n_dens = 3 * width_x + 2
    bf16, f32 = jnp.bfloat16, jnp.float32
    args = (*pieces, mats, wfirst, whead)
    return pl.pallas_call(
        functools.partial(chain_kernel, width_x, width_y),
        out_shape=(
            jax.ShapeDtypeStruct((3, width_x, width_y, depth_z), bf16),
            jax.ShapeDtypeStruct((CH, 512), f32),
        ),
        in_specs=[pl.BlockSpec(memory_space=pltpu.VMEM)] * len(args),
        out_specs=(pl.BlockSpec(memory_space=pltpu.VMEM),) * 2,
        scratch_shapes=[
            pltpu.VMEM((width_x + 4, 3 * full_y, depth_z), bf16),
            pltpu.VMEM((n_dens * 3 * full_y, depth_z), bf16),
            pltpu.VMEM((2 * n_dens - 6, depth_z, 3 * lanes), bf16),
            pltpu.VMEM((width_x, depth_z, lanes), bf16),
            pltpu.VMEM((2 * n_dens - 14, depth_z, 3 * lanes), bf16),
            pltpu.VMEM((width_x, depth_z, own), f32),
            pltpu.VMEM((width_x + 2, depth_z, lanes), f32),
            pltpu.VMEM((3, lanes, 3 * lanes), f32),
        ],
        compiler_params=pltpu.CompilerParams(vmem_limit_bytes=36 * 1024 * 1024),
        name="chain",
    )(*args)


def passed_along(x, axis, by):
    devices = lax.axis_size(axis)
    return lax.ppermute(x, axis, [(i, (i + by) % devices) for i in range(devices)])


def exchanged(x, axis, mask):
    return lax.ppermute(x, axis, [(i, i ^ mask) for i in range(lax.axis_size(axis))])


def summed(total):
    stride, chips = 1, lax.axis_size("slab")
    while stride < chips:
        if chips // stride >= 4:
            got = [exchanged(total, "slab", stride * i) for i in (1, 2, 3)]
            total = (total + got[0]) + (got[1] + got[2])
            stride *= 4
        else:
            total = total + exchanged(total, "slab", stride)
            stride *= 2
    return total, exchanged(total, "sub", 1)


def finish_kernel(loss_scale, mine_ref, theirs_ref, first_ref, mid_ref, last_ref, head_ref):
    first_core = lax.axis_index("sub") == 0
    taps = 27 * CH
    mine, theirs = mine_ref[...] * loss_scale, theirs_ref[...] * loss_scale
    mid = jnp.where(first_core, theirs, mine)
    last = jnp.where(first_core, mine, theirs)
    mid_ref[...] = mid[:, :taps]
    last_ref[...] = last[:, :taps]
    both = mine[:, 384:] + theirs[:, 384:]
    first_ref[...] = pltpu.roll(both, 80, axis=1)[:, :27]
    head_ref[...] = pltpu.roll(both, 48, axis=1)[:3, : 2 * CH]


def finished(mine, theirs, loss_scale):
    f32 = jnp.float32
    return pl.pallas_call(
        functools.partial(finish_kernel, loss_scale),
        out_shape=(
            jax.ShapeDtypeStruct((CH, 27), f32),
            jax.ShapeDtypeStruct((CH, 27 * CH), f32),
            jax.ShapeDtypeStruct((CH, 27 * CH), f32),
            jax.ShapeDtypeStruct((3, 2 * CH), f32),
        ),
        in_specs=[pl.BlockSpec(memory_space=pltpu.VMEM)] * 2,
        out_specs=(pl.BlockSpec(memory_space=pltpu.VMEM),) * 4,
        compiler_params=pltpu.CompilerParams(vmem_limit_bytes=4 * 1024 * 1024),
        name="finish",
    )(mine, theirs)


def per_device(part_cells, part_offsets, part_counts, w_first, w_mid, w_last, w_head, cotangent):
    n_slab = lax.axis_size("slab")
    n_sub = lax.axis_size("sub")
    axes = ("slab", "sub")
    width_x = cotangent.shape[1]
    width_y = cotangent.shape[2]
    depth_z = cotangent.shape[3]
    cap = part_cells.shape[2]

    def outward(x, by):
        pairs = []
        for i in range(n_slab):
            pairs.append((i * n_sub, (i + by) % n_slab * n_sub))
            pairs.append((i * n_sub + 1, (i - by) % n_slab * n_sub + 1))
        return lax.ppermute(x, axes, pairs)

    raw = side_by_side(w_first, w_mid, w_last, w_head)
    words = packed_slots(part_cells[0], part_offsets[0], part_counts, width_x, width_y, depth_z)
    ct_other = exchanged(cotangent, "sub", 1)
    words, ct_other = lax.optimization_barrier((words, ct_other))
    ct_middle, ct_edge = edges(cotangent, ct_other)
    ct_mine = outward(ct_edge, 1)
    ct_theirs = exchanged(ct_mine, "sub", 1)
    got = lax.all_to_all(words, axes, split_axis=0, concat_axis=0, tiled=True)
    own = deposit(got, ct_mine, raw, cap, width_x, width_y, depth_z)
    near, far = combined(own, exchanged(own, "sub", 1), width_x, width_y)
    mats, wfirst, whead = weight_matrices(raw, far, n_sub * width_y)
    near_mine, far_mine, whead = lax.optimization_barrier((outward(near, 1), outward(far, 2), whead))
    near_theirs, far_theirs = exchanged(near_mine, "sub", 1), exchanged(far_mine, "sub", 1)
    pieces = (near, near_mine, near_theirs, far_mine, far_theirs, ct_middle, ct_mine, ct_theirs)
    force, mine = chain(pieces, mats, wfirst, whead, width_x, width_y, depth_z)
    loss_scale = 1.0 / math.sqrt(width_x * n_slab * width_y * n_sub * depth_z)
    return (force, *finished(*summed(mine), loss_scale))


def solution(mesh):
    in_specs = (
        P(("slab", "sub"), None, None),
        P(("slab", "sub"), None, None, None),
        P(("slab", "sub"), None),
        P(),
        P(),
        P(),
        P(),
        P(None, "slab", "sub", None),
    )
    out_specs = (P(None, "slab", "sub", None), P(), P(), P(), P())
    return jax.shard_map(
        per_device, mesh=mesh, in_specs=in_specs, out_specs=out_specs, check_vma=False
    )
```

```python
import functools
import math

import jax
import jax.numpy as jnp
from jax import lax
from jax.experimental import pallas as pl
from jax.experimental.pallas import tpu as pltpu
from jax.sharding import PartitionSpec as P

BITS = 21
STEPS = 1 << BITS


def pack_kernel(dead, cells_hbm, offsets_hbm, counts_hbm, words_ref, cells_ref, offsets_ref, counts_ref, sems):
    dests, cap = cells_ref.shape
    copies = [
        pltpu.make_async_copy(source, target, sems.at[i])
        for i, (source, target) in enumerate(
            ((counts_hbm, counts_ref), (cells_hbm, cells_ref), (offsets_hbm, offsets_ref))
        )
    ]
    for copy in copies:
        copy.start()
    for copy in copies:
        copy.wait()
    eye = lax.broadcasted_iota(jnp.int32, (dests, dests), 0) == lax.broadcasted_iota(jnp.int32, (dests, dests), 1)
    counts = jnp.where(eye, counts_ref[...].astype(jnp.float32), 0.0)
    counts = jnp.sum(counts, axis=1, keepdims=True).astype(jnp.int32)
    live = lax.broadcasted_iota(jnp.int32, (dests, cap), 1) < counts
    code = jnp.where(live, cells_ref[...], dead)
    fixed = [
        jnp.minimum((offsets_ref[i] * STEPS + 0.5).astype(jnp.int32), STEPS - 1) for i in range(3)
    ]
    first = fixed[0] | (fixed[2] << BITS)
    second = fixed[1] | ((fixed[2] >> (32 - BITS)) << BITS)
    codes = code[:, : cap // 2] | (code[:, cap // 2 :] << 16)
    for dest in range(dests):
        words_ref[dest, :, 0:cap] = first[dest : dest + 1]
        words_ref[dest, :, cap : 2 * cap] = second[dest : dest + 1]
        words_ref[dest, :, 2 * cap :] = codes[dest : dest + 1]


def packed_slots(cells, offsets, counts, width_x, width_y, depth_z):
    dests, cap = cells.shape
    return pl.pallas_call(
        functools.partial(pack_kernel, 2 * width_x * width_y * depth_z),
        out_shape=jax.ShapeDtypeStruct((dests, 1, 5 * cap // 2), jnp.int32),
        in_specs=[pl.BlockSpec(memory_space=pltpu.HBM)] * 3,
        out_specs=pl.BlockSpec(memory_space=pltpu.VMEM),
        scratch_shapes=[
            pltpu.VMEM((dests, cap), jnp.int32),
            pltpu.VMEM((3, dests, cap), jnp.float32),
            pltpu.VMEM((1, dests), jnp.int32),
            pltpu.SemaphoreType.DMA((3,)),
        ],
        compiler_params=pltpu.CompilerParams(vmem_limit_bytes=60 * 1024 * 1024),
        name="pack",
    )(cells, offsets.transpose(1, 0, 2), counts)


def deposit_kernel(width_x, width_y, depth_z, cap, words_ref, after_ref, late_ref, out_ref, acc_ref):
    rows = out_ref.shape[0]
    acc_ref[...] = jnp.zeros_like(acc_ref)
    slot_rows = cap // 128
    source_rows = slot_rows * 5 // 2
    group = 16 // slot_rows
    row_id = lax.broadcasted_iota(jnp.int32, (8, 128), 0)
    z_id = lax.broadcasted_iota(jnp.int32, (depth_z, 128), 0).astype(jnp.float32).astype(jnp.bfloat16)
    one, zero = jnp.bfloat16(1.0), jnp.bfloat16(0.0)

    def body(i, carry):
        block = words_ref[pl.ds(pl.multiple_of(i * group * source_rows, 8), group * source_rows), :]

        def gathered(start, length):
            parts = [block[k * source_rows + start : k * source_rows + start + length] for k in range(group)]
            return parts

        first = jnp.concatenate(gathered(0, slot_rows), axis=0)
        second = jnp.concatenate(gathered(slot_rows, slot_rows), axis=0)
        halves = gathered(2 * slot_rows, slot_rows // 2)
        code = jnp.concatenate([part for half in halves for part in (half & 0xFFFF, (half >> 16) & 0xFFFF)], axis=0)
        inv = 1.0 / STEPS
        fixed_z = ((first >> BITS) & ((1 << (32 - BITS)) - 1)) | ((second >> BITS) << (32 - BITS))
        frac_x = (first & (STEPS - 1)).astype(jnp.float32) * inv
        frac_y = (second & (STEPS - 1)).astype(jnp.float32) * inv
        frac_z = fixed_z.astype(jnp.float32) * inv
        cell_z = (code % depth_z).astype(jnp.float32)
        column = code // depth_z
        cell_y = column % width_y
        cell_x = column // width_y
        past = jnp.where(cell_y == width_y - 1, frac_y, 0.0)
        rest_x, rest_y, rest_z = 1.0 - frac_x, 1.0 - frac_y, 1.0 - frac_z
        weights, hot = [], []
        for k in range(16):
            row = slice(k, k + 1)
            at_y, at_x = cell_y[row], cell_x[row]
            wy = jnp.where(at_y == row_id, rest_y[row], jnp.where(at_y + 1 == row_id, frac_y[row], 0.0))
            wx = jnp.where(at_x == row_id, rest_x[row], jnp.where(at_x + 1 == row_id, frac_x[row], 0.0))
            parts = [wx[x : x + 1] * wy for x in range(width_x + 1)] + [wx * past[row]]
            area = jnp.concatenate(parts, axis=0)
            low, high = area * rest_z[row], area * frac_z[row]
            low_a, high_a = low.astype(jnp.bfloat16), high.astype(jnp.bfloat16)
            low_b = (low - low_a.astype(jnp.float32)).astype(jnp.bfloat16)
            high_b = (high - high_a.astype(jnp.float32)).astype(jnp.bfloat16)
            weights.append(jnp.concatenate([low_a, low_b, high_a, high_b], axis=0))
            at_z = jnp.broadcast_to(cell_z[row], (depth_z, 128)).astype(jnp.bfloat16)
            hot.append(jnp.where(at_z == z_id, one, zero))
        acc_ref[...] += lax.dot_general(
            jnp.concatenate(weights, axis=1),
            jnp.concatenate(hot, axis=1),
            (((1,), (1,)), ((), ())),
            preferred_element_type=jnp.float32,
        )
        return carry

    lax.fori_loop(0, words_ref.shape[0] // (group * source_rows), body, 0, unroll=16)
    low = acc_ref[0:rows] + acc_ref[rows : 2 * rows]
    high = acc_ref[2 * rows : 3 * rows] + acc_ref[3 * rows : 4 * rows]
    out_ref[...] = low + pltpu.roll(high, 1, axis=1)


def deposit(words, after, late, cap, width_x, width_y, depth_z):
    rows = (width_x + 1) * width_y + 8
    return pl.pallas_call(
        functools.partial(deposit_kernel, width_x, width_y, depth_z, cap),
        out_shape=jax.ShapeDtypeStruct((rows, depth_z), jnp.float32),
        in_specs=[pl.BlockSpec(memory_space=pltpu.VMEM)] * 3,
        out_specs=pl.BlockSpec(memory_space=pltpu.VMEM),
        scratch_shapes=[pltpu.VMEM((4 * rows, depth_z), jnp.float32)],
        compiler_params=pltpu.CompilerParams(vmem_limit_bytes=16 * 1024 * 1024),
        name="deposit",
    )(words.reshape(-1, 128), after, late)


def combine_kernel(width_x, width_y, own_ref, other_ref, near_ref, far_ref):
    full_y = 2 * width_y
    spill = (width_x + 1) * width_y
    top = lax.broadcasted_iota(jnp.int32, (width_y, own_ref.shape[1]), 0) == 0
    planes = []
    for x in range(width_x + 1):
        rows, edge = slice(x * width_y, (x + 1) * width_y), slice(spill + x, spill + x + 1)
        upper = own_ref[rows] + jnp.where(top, other_ref[edge], 0.0)
        lower = other_ref[rows] + jnp.where(top, own_ref[edge], 0.0)
        near_ref[x * full_y : x * full_y + width_y] = upper
        near_ref[x * full_y + width_y : (x + 1) * full_y] = lower
        planes.append((upper, lower))
    upward = lax.axis_index("sub") == 0
    for i, (up, down) in enumerate(((width_x - 1, 0), (width_x, 0))):
        for half in range(2):
            start = i * full_y + half * width_y
            far_ref[start : start + width_y] = jnp.where(upward, planes[up][half], planes[down][half])


def combined(own, other, width_x, width_y):
    depth_z = own.shape[1]
    full_y = 2 * width_y
    return pl.pallas_call(
        functools.partial(combine_kernel, width_x, width_y),
        out_shape=(
            jax.ShapeDtypeStruct(((width_x + 1) * full_y, depth_z), jnp.float32),
            jax.ShapeDtypeStruct((2 * full_y, depth_z), jnp.float32),
        ),
        in_specs=[pl.BlockSpec(memory_space=pltpu.VMEM)] * 2,
        out_specs=(pl.BlockSpec(memory_space=pltpu.VMEM),) * 2,
        compiler_params=pltpu.CompilerParams(vmem_limit_bytes=4 * 1024 * 1024),
        name="combine",
    )(own, other)


CH = 16


def dot(a, b, dims=((1,), (0,))):
    return lax.dot_general(a, b, (dims, ((), ())), preferred_element_type=jnp.float32)


def iota(shape, axis):
    return lax.broadcasted_iota(jnp.int32, shape, axis)


def weights_kernel(
    full_y, raw_ref, after_ref, mats_ref, wfirst_ref, whead_ref, square, taps_ref
):
    lanes = full_y * CH
    f32, bf16 = jnp.float32, jnp.bfloat16
    slot = iota((CH, 128), 1) // CH

    def turned(x, by):
        return x if by % 128 == 0 else pltpu.roll(x, by % 128, axis=1)

    square[...] = jnp.zeros_like(square)
    for which in range(2):
        square[0:CH, :] = raw_ref[:, which * 512 : (which + 1) * 512].astype(f32)
        flipped = jnp.transpose(square[...])
        for dx in range(3):
            for dz in range(3):
                ahead = back = jnp.zeros((CH, 128), f32)
                for dy in range(3):
                    start = (dx * 9 + dy * 3 + dz) * CH
                    ahead = ahead + turned(flipped[start : start + CH], dy * CH)
                    block = start // 128 * 128
                    picked = jnp.where(slot == (start - block) // CH, square[0:CH, block : block + 128], 0.0)
                    back = back + turned(picked, dy * CH - (start - block))
                rows = slice((dx * 3 + dz) * CH, (dx * 3 + dz + 1) * CH)
                taps_ref[which, rows, :] = ahead.astype(bf16)
                taps_ref[2 + which, rows, :] = back.astype(bf16)

    row, lane = iota((128, lanes), 0), iota((128, lanes), 1)
    same = row % CH == lane % CH
    shift, lane_y = row // CH - 1, lane // CH

    def body(y, carry):
        forward = jnp.where(same & (lane_y == (y - shift + full_y) % full_y), 1.0, 0.0).astype(bf16)
        back = jnp.where(same & (lane_y == (y + shift + full_y) % full_y), 1.0, 0.0).astype(bf16)
        for which in range(4):
            spread = dot(taps_ref[which], forward if which < 2 else back).astype(bf16)
            for dx in range(3):
                for dz in range(3):
                    tap = dx * 3 + dz if which < 2 else (2 - dx) * 3 + 2 - dz
                    start = pl.multiple_of(dz * lanes + y * CH, CH)
                    mats_ref[which, dx, pl.ds(start, CH), :] = spread[tap * CH : (tap + 1) * CH]
        return carry

    lax.fori_loop(0, full_y, body, 0, unroll=4)

    rows = 9 * full_y
    at_y, at_lane = iota((rows, lanes), 0) % full_y, iota((rows, lanes), 1) // CH
    square[...] = jnp.zeros_like(square)
    square[0:CH, 0:128] = raw_ref[:, 1024:1152].astype(f32)
    flipped = jnp.transpose(square[:, 0:128])
    spread_rows = []
    for dx in range(3):
        for dz in range(3):
            line = jnp.zeros((1, 128), f32)
            for dy in range(3):
                tap = dx * 9 + dy * 3 + dz
                line = line + turned(flipped[tap : tap + 1], dy * CH)
            spread_rows.append(jnp.broadcast_to(line, (full_y, 128)))
    first = jnp.concatenate(spread_rows, axis=0).astype(bf16)
    total = jnp.zeros((rows, lanes), f32)
    for dy in range(3):
        pick = jnp.where(same & (row // CH == dy), 1.0, 0.0).astype(bf16)
        total = jnp.where(at_y == (at_lane + dy - 1 + full_y) % full_y, dot(first, pick), total)
    wfirst_ref[...] = total.astype(bf16)

    rows = 3 * full_y
    at_y, at_lane = iota((rows, lanes), 0) % full_y, iota((rows, lanes), 1) // CH
    square[...] = jnp.zeros_like(square)
    square[0:CH, 0:128] = raw_ref[:, 1152:1280].astype(f32)
    head = [jnp.broadcast_to(square[k : k + 1, 0:128], (full_y, 128)) for k in range(3)]
    head = jnp.concatenate(head, axis=0).astype(bf16)
    for half in range(2):
        pick = jnp.where(row == lane % CH + half * CH, 1.0, 0.0).astype(bf16)
        whead_ref[half] = jnp.where(at_y == at_lane, dot(head, pick), 0.0).astype(bf16)


def side_by_side(w_first, w_mid, w_last, w_head):
    def widened(w, columns):
        return jnp.pad(w, ((0, CH - w.shape[0]), (0, columns - w.shape[1])))

    return jnp.concatenate([widened(w_mid, 512), widened(w_last, 512), widened(w_first, 128), widened(w_head, 128)], axis=1)


def weight_matrices(raw, after, full_y):
    lanes = full_y * CH
    return pl.pallas_call(
        functools.partial(weights_kernel, full_y),
        out_shape=(
            jax.ShapeDtypeStruct((4, 3, 3 * lanes, lanes), jnp.bfloat16),
            jax.ShapeDtypeStruct((9 * full_y, lanes), jnp.bfloat16),
            jax.ShapeDtypeStruct((2, 3 * full_y, lanes), jnp.bfloat16),
        ),
        in_specs=[pl.BlockSpec(memory_space=pltpu.VMEM)] * 2,
        out_specs=(pl.BlockSpec(memory_space=pltpu.VMEM),) * 3,
        scratch_shapes=[pltpu.VMEM((128, 512), jnp.float32), pltpu.VMEM((4, 9 * CH, 128), jnp.bfloat16)],
        compiler_params=pltpu.CompilerParams(vmem_limit_bytes=16 * 1024 * 1024),
        cost_estimate=pl.CostEstimate(flops=2 * 4 * 9 * CH * 128 * lanes * full_y, bytes_accessed=8 << 20, transcendentals=0),
        name="weights",
    )(raw, after)


def edges_kernel(width_x, width_y, own_ref, other_ref, middle_ref, edge_ref):
    full_y = 2 * width_y
    upward = lax.axis_index("sub") == 0
    for k in range(3):
        rows = slice(k * full_y, (k + 1) * full_y)
        planes = []
        for x in range(width_x):
            both = [own_ref[k, x].astype(jnp.float32), other_ref[k, x].astype(jnp.float32)]
            planes.append(jnp.concatenate(both, axis=0))
            middle_ref[x, rows] = planes[x].astype(jnp.bfloat16)
        for i in range(2):
            edge_ref[i, rows] = jnp.where(upward, planes[width_x - 2 + i], planes[i]).astype(jnp.bfloat16)


def edges(own, other):
    _, width_x, width_y, depth_z = own.shape
    return pl.pallas_call(
        functools.partial(edges_kernel, width_x, width_y),
        out_shape=(
            jax.ShapeDtypeStruct((width_x, 6 * width_y, depth_z), jnp.bfloat16),
            jax.ShapeDtypeStruct((2, 6 * width_y, depth_z), jnp.bfloat16),
        ),
        in_specs=[pl.BlockSpec(memory_space=pltpu.VMEM)] * 2,
        out_specs=(pl.BlockSpec(memory_space=pltpu.VMEM),) * 2,
        compiler_params=pltpu.CompilerParams(vmem_limit_bytes=4 * 1024 * 1024),
        name="edges",
    )(own, other)


def sigmoid(v):
    return 0.5 + 0.5 * jnp.tanh(0.5 * v)


def chain_kernel(
    width_x,
    width_y,
    near_ref,
    near_mine,
    near_theirs,
    far_mine,
    far_theirs,
    ct_middle,
    ct_mine,
    ct_theirs,
    mats_ref,
    wfirst_ref,
    whead_ref,
    force_ref,
    mine_ref,
    ct_ref,
    dens,
    one,
    two,
    three,
    g_three,
    g_two,
    pre_one,
    pre_two,
    wg,
):
    full_y = 2 * width_y
    depth = ct_ref.shape[2]
    lanes = full_y * CH
    own = width_y * CH
    first_core = lax.axis_index("sub") == 0

    def turned(ref, plane):
        start = plane * full_y
        return jnp.concatenate([ref[start + width_y : start + full_y], ref[start : start + width_y]], axis=0)

    def straight(ref, plane):
        return ref[plane * full_y : (plane + 1) * full_y]

    planes = [straight(near_ref, x) for x in range(width_x + 1)]
    below = [jnp.where(first_core, straight(near_mine, x), turned(near_theirs, x)) for x in range(width_x + 1)]
    above = [jnp.where(first_core, turned(near_theirs, x), straight(near_mine, x)) for x in range(width_x + 1)]
    tail = [jnp.where(first_core, straight(far_mine, x), turned(far_theirs, x)) for x in range(2)]
    ahead = jnp.where(first_core, turned(far_theirs, 0), straight(far_mine, 0))
    column = [tail[0], tail[1] + below[0], *below[1:width_x], below[width_x] + planes[0], *planes[1:width_x]]
    column = column + [planes[width_x] + above[0], *above[1:width_x], above[width_x] + ahead]
    n_dens = 3 * width_x + 2
    for j in range(n_dens):
        plane = column[j]
        around = [pltpu.roll(plane, 1, axis=1), plane, pltpu.roll(plane, depth - 1, axis=1)]
        dens[3 * full_y * j : 3 * full_y * (j + 1)] = jnp.concatenate(around, axis=0).astype(jnp.bfloat16)

    for x in range(width_x):
        ct_ref[x + 2] = ct_middle[x]
    for x in range(2):
        mine, theirs = ct_mine[x].astype(jnp.float32), ct_theirs[x].astype(jnp.float32)
        halves = [theirs[i * width_y : (i + 1) * width_y] for i in (1, 0, 3, 2, 5, 4)]
        theirs = jnp.concatenate(halves, axis=0)
        ct_ref[x] = jnp.where(first_core, mine, theirs).astype(jnp.bfloat16)
        ct_ref[x + 2 + width_x] = jnp.where(first_core, theirs, mine).astype(jnp.bfloat16)

    def window(x):
        return dens[pl.ds(pl.multiple_of(3 * full_y * x, 3 * full_y), 9 * full_y), :]

    def put(ref, x, field):
        ref[x, :, 0:lanes] = pltpu.roll(field, 1, axis=0).astype(jnp.bfloat16)
        ref[x, :, lanes : 2 * lanes] = field.astype(jnp.bfloat16)
        ref[x, :, 2 * lanes : 3 * lanes] = pltpu.roll(field, depth - 1, axis=0).astype(jnp.bfloat16)

    def conv(ref, x, which):
        total = None
        for dx in range(3):
            part = dot(ref[x + dx : x + dx + 2].reshape(2 * depth, 3 * lanes), mats_ref[which, dx])
            total = part if total is None else total + part
        return total.reshape(2, depth, lanes)

    def slope(v):
        s = sigmoid(v)
        return s * (1.0 + v * (1.0 - s))

    def first_plane(x):
        v = dot(window(x), wfirst_ref[...], ((0,), (0,)))
        if 0 <= x - 4 < width_x:
            pre_one[x - 4] = v[:, 0:own]
        put(one, x, v * sigmoid(v))

    def second_done(i, both):
        for k in range(2):
            v, x = both[k], 2 * i + k
            if 0 <= x - 2 < width_x + 2:
                pre_two[x - 2] = v
            put(two, x, v * sigmoid(v))

    def third_done(i, both):
        for k in range(2):
            v, x = both[k], 2 * i + k
            s = sigmoid(v)
            if 0 <= x - 2 < width_x:
                three[x - 2] = (v * s).astype(jnp.bfloat16)
            back = dot(ct_ref[x], whead_ref[0], ((0,), (0,)))
            put(g_three, x, back * (s * (1.0 + v * (1.0 - s))))

    def back_done(i, both):
        for k in range(2):
            x = 2 * i + k
            put(g_two, x, both[k] * slope(pre_two[x]))

    layers = ((one, 0, second_done), (two, 1, third_done), (g_three, 3, back_done))
    pairs = [(n_dens - 4 - 2 * layer) // 2 for layer in range(3)]
    order = sorted(
        ((i + 2.6 * layer, layer, i) for layer in range(3) for i in range(pairs[layer])),
    )
    firsts_done = 0
    waiting = None
    for _, layer, i in order:
        if layer == 0:
            while firsts_done < 2 * i + 4:
                first_plane(firsts_done)
                firsts_done += 1
        elif waiting is not None and waiting[0] == layer - 1 and waiting[1] <= i + 1:
            layers[waiting[0]][2](waiting[1], waiting[2])
            waiting = None
        ref, which, done = layers[layer]
        both = conv(ref, 2 * i, which)
        if waiting is not None:
            layers[waiting[0]][2](waiting[1], waiting[2])
        waiting = (layer, i, both)
    layers[waiting[0]][2](waiting[1], waiting[2])

    ct_own = jnp.concatenate([ct_ref[x + 2] for x in range(width_x)], axis=1)
    heads = [
        dot(ct_own, three[:, :, 0:own].reshape(width_x * depth, own)),
        dot(ct_own, one[4 : 4 + width_x, :, lanes : lanes + own].reshape(width_x * depth, own)),
    ]
    for x in range(width_x):
        h_three, h_one = three[x], one[x + 4, :, lanes : 2 * lanes]
        rows = dot(h_three, whead_ref[0], ((1,), (1,))) + dot(h_one, whead_ref[1], ((1,), (1,)))
        rows = jnp.transpose(rows)
        for k in range(3):
            force_ref[k, x] = rows[k * full_y : k * full_y + width_y].astype(jnp.bfloat16)

    across = []
    for x in range(width_x):
        middle = slice(lanes, 2 * lanes)
        across.append(jnp.transpose(jnp.where(first_core, g_three[x + 2, :, middle], g_two[x + 1, :, middle])))
    across = jnp.concatenate(across, axis=1)
    for dx in range(3):
        field = jnp.where(first_core, two[2 + dx : 2 + dx + width_x], one[3 + dx : 3 + dx + width_x])
        wg[dx] = dot(across, field.reshape(width_x * depth, 3 * lanes))
    grad_one = []
    for i in range(width_x // 2):
        total = jnp.zeros((depth, 2 * own), jnp.float32)
        for plane in range(4):
            nothing = jnp.zeros((3 * lanes, own), jnp.bfloat16)
            left = mats_ref[2, plane, :, 0:own] if plane < 3 else nothing
            right = mats_ref[2, plane - 1, :, 0:own] if plane > 0 else nothing
            total = total + dot(g_two[2 * i + plane], jnp.concatenate([left, right], axis=1))
        for k in range(2):
            x = 2 * i + k
            back = total[:, k * own : (k + 1) * own] + dot(ct_ref[x + 2], whead_ref[1, :, 0:own], ((0,), (0,)))
            grad_one.append((back * slope(pre_one[x])).astype(jnp.bfloat16))
    windows = jnp.concatenate([window(x + 4) for x in range(width_x)], axis=1)
    firsts = dot(windows, jnp.concatenate(grad_one, axis=0))

    lane = iota((CH, 128), 1)
    blocks = [jnp.zeros((CH, 128), jnp.float32) for _ in range(4)]
    for dx in range(3):
        for dz in range(3):
            lined = jnp.zeros((CH, lanes), jnp.float32)
            for y in range(full_y):
                piece = wg[dx, y * CH : (y + 1) * CH, dz * lanes : (dz + 1) * lanes]
                turn = (lanes - CH * (y - 1)) % lanes
                lined = lined + (piece if turn == 0 else pltpu.roll(piece, turn, axis=1))
            for dy in range(3):
                target = (dx * 9 + dy * 3 + dz) * CH
                turn = (target - dy * CH) % 128
                piece = jnp.where(lane // CH == dy, lined[:, 0:128], 0.0)
                blocks[target // 128] += piece if turn == 0 else pltpu.roll(piece, turn, axis=1)
    def folded(rows):
        for turn in (64, 32, 16):
            rows = rows + pltpu.roll(rows, turn, axis=1)
        return rows

    at_y, at_lane = iota((full_y, own), 0), iota((full_y, own), 1) // CH
    first_rows = []
    for dx in range(3):
        for dy in range(3):
            match = at_y == (at_lane + dy - 1 + full_y) % full_y
            for dz in range(3):
                tap = (dx * 3 + dz) * full_y
                part = jnp.where(match, firsts[tap : tap + full_y, :], 0.0)
                first_rows.append(jnp.sum(part, axis=0, keepdims=True))
    first = folded(jnp.concatenate(first_rows + [jnp.zeros((5, own), jnp.float32)], axis=0))
    gap = jnp.zeros((48, own), jnp.float32)
    blocks[3] += jnp.transpose(jnp.concatenate([gap, first, gap], axis=0))[0:CH]
    for half in range(2):
        rows = []
        for k in range(3):
            part = jnp.where(at_y == at_lane, heads[half][k * full_y : (k + 1) * full_y], 0.0)
            rows.append(jnp.sum(part, axis=0, keepdims=True))
        head = folded(jnp.concatenate(rows + [jnp.zeros((CH - 3, own), jnp.float32)], axis=0))
        blocks[3] += jnp.where(lane // CH == 5 + half, head, 0.0)
    for block in range(4):
        mine_ref[:, block * 128 : (block + 1) * 128] = blocks[block]


def chain(pieces, mats, wfirst, whead, width_x, width_y, depth_z):
    full_y = 2 * width_y
    lanes, own = full_y * CH, width_y * CH
    n_dens = 3 * width_x + 2
    bf16, f32 = jnp.bfloat16, jnp.float32
    args = (*pieces, mats, wfirst, whead)
    return pl.pallas_call(
        functools.partial(chain_kernel, width_x, width_y),
        out_shape=(
            jax.ShapeDtypeStruct((3, width_x, width_y, depth_z), bf16),
            jax.ShapeDtypeStruct((CH, 512), f32),
        ),
        in_specs=[pl.BlockSpec(memory_space=pltpu.VMEM)] * len(args),
        out_specs=(pl.BlockSpec(memory_space=pltpu.VMEM),) * 2,
        scratch_shapes=[
            pltpu.VMEM((width_x + 4, 3 * full_y, depth_z), bf16),
            pltpu.VMEM((n_dens * 3 * full_y, depth_z), bf16),
            pltpu.VMEM((n_dens - 2, depth_z, 3 * lanes), bf16),
            pltpu.VMEM((n_dens - 4, depth_z, 3 * lanes), bf16),
            pltpu.VMEM((width_x, depth_z, lanes), bf16),
            pltpu.VMEM((n_dens - 6, depth_z, 3 * lanes), bf16),
            pltpu.VMEM((n_dens - 8, depth_z, 3 * lanes), bf16),
            pltpu.VMEM((width_x, depth_z, own), f32),
            pltpu.VMEM((width_x + 2, depth_z, lanes), f32),
            pltpu.VMEM((3, lanes, 3 * lanes), f32),
        ],
        compiler_params=pltpu.CompilerParams(vmem_limit_bytes=36 * 1024 * 1024),
        name="chain",
    )(*args)


def passed_along(x, axis, by):
    devices = lax.axis_size(axis)
    return lax.ppermute(x, axis, [(i, (i + by) % devices) for i in range(devices)])


def exchanged(x, axis, mask):
    return lax.ppermute(x, axis, [(i, i ^ mask) for i in range(lax.axis_size(axis))])


def summed(total):
    stride, chips = 1, lax.axis_size("slab")
    while stride < chips:
        if chips // stride >= 4:
            got = [exchanged(total, "slab", stride * i) for i in (1, 2, 3)]
            total = (total + got[0]) + (got[1] + got[2])
            stride *= 4
        else:
            total = total + exchanged(total, "slab", stride)
            stride *= 2
    return total, exchanged(total, "sub", 1)


def finish_kernel(loss_scale, mine_ref, theirs_ref, first_ref, mid_ref, last_ref, head_ref):
    first_core = lax.axis_index("sub") == 0
    taps = 27 * CH
    mine, theirs = mine_ref[...] * loss_scale, theirs_ref[...] * loss_scale
    mid = jnp.where(first_core, theirs, mine)
    last = jnp.where(first_core, mine, theirs)
    mid_ref[...] = mid[:, :taps]
    last_ref[...] = last[:, :taps]
    both = mine[:, 384:] + theirs[:, 384:]
    first_ref[...] = pltpu.roll(both, 80, axis=1)[:, :27]
    head_ref[...] = pltpu.roll(both, 48, axis=1)[:3, : 2 * CH]


def finished(mine, theirs, loss_scale):
    f32 = jnp.float32
    return pl.pallas_call(
        functools.partial(finish_kernel, loss_scale),
        out_shape=(
            jax.ShapeDtypeStruct((CH, 27), f32),
            jax.ShapeDtypeStruct((CH, 27 * CH), f32),
            jax.ShapeDtypeStruct((CH, 27 * CH), f32),
            jax.ShapeDtypeStruct((3, 2 * CH), f32),
        ),
        in_specs=[pl.BlockSpec(memory_space=pltpu.VMEM)] * 2,
        out_specs=(pl.BlockSpec(memory_space=pltpu.VMEM),) * 4,
        compiler_params=pltpu.CompilerParams(vmem_limit_bytes=4 * 1024 * 1024),
        name="finish",
    )(mine, theirs)


def per_device(part_cells, part_offsets, part_counts, w_first, w_mid, w_last, w_head, cotangent):
    n_slab = lax.axis_size("slab")
    n_sub = lax.axis_size("sub")
    axes = ("slab", "sub")
    width_x = cotangent.shape[1]
    width_y = cotangent.shape[2]
    depth_z = cotangent.shape[3]
    cap = part_cells.shape[2]

    def outward(x, by):
        pairs = []
        for i in range(n_slab):
            pairs.append((i * n_sub, (i + by) % n_slab * n_sub))
            pairs.append((i * n_sub + 1, (i - by) % n_slab * n_sub + 1))
        return lax.ppermute(x, axes, pairs)

    raw = side_by_side(w_first, w_mid, w_last, w_head)
    words = packed_slots(part_cells[0], part_offsets[0], part_counts, width_x, width_y, depth_z)
    ct_other = exchanged(cotangent, "sub", 1)
    words, ct_other = lax.optimization_barrier((words, ct_other))
    ct_middle, ct_edge = edges(cotangent, ct_other)
    ct_mine = outward(ct_edge, 1)
    ct_theirs = exchanged(ct_mine, "sub", 1)
    got = lax.all_to_all(words, axes, split_axis=0, concat_axis=0, tiled=True)
    own = deposit(got, ct_mine, raw, cap, width_x, width_y, depth_z)
    near, far = combined(own, exchanged(own, "sub", 1), width_x, width_y)
    mats, wfirst, whead = weight_matrices(raw, far, n_sub * width_y)
    near_mine, far_mine, whead = lax.optimization_barrier((outward(near, 1), outward(far, 2), whead))
    near_theirs, far_theirs = exchanged(near_mine, "sub", 1), exchanged(far_mine, "sub", 1)
    pieces = (near, near_mine, near_theirs, far_mine, far_theirs, ct_middle, ct_mine, ct_theirs)
    force, mine = chain(pieces, mats, wfirst, whead, width_x, width_y, depth_z)
    loss_scale = 1.0 / math.sqrt(width_x * n_slab * width_y * n_sub * depth_z)
    return (force, *finished(*summed(mine), loss_scale))


def solution(mesh):
    in_specs = (
        P(("slab", "sub"), None, None),
        P(("slab", "sub"), None, None, None),
        P(("slab", "sub"), None),
        P(),
        P(),
        P(),
        P(),
        P(None, "slab", "sub", None),
    )
    out_specs = (P(None, "slab", "sub", None), P(), P(), P(), P())
    return jax.shard_map(
        per_device, mesh=mesh, in_specs=in_specs, out_specs=out_specs, check_vma=False
    )
```

```python
import functools
import math

import jax
import jax.numpy as jnp
from jax import lax
from jax.experimental import pallas as pl
from jax.experimental.pallas import tpu as pltpu
from jax.sharding import PartitionSpec as P

BITS = 21
STEPS = 1 << BITS


def pack_kernel(dead, cells_hbm, offsets_hbm, counts_hbm, words_ref, cells_ref, offsets_ref, counts_ref, sems):
    dests, cap = cells_ref.shape
    copies = [
        pltpu.make_async_copy(source, target, sems.at[i])
        for i, (source, target) in enumerate(
            ((counts_hbm, counts_ref), (cells_hbm, cells_ref), (offsets_hbm, offsets_ref))
        )
    ]
    for copy in copies:
        copy.start()
    for copy in copies:
        copy.wait()
    eye = lax.broadcasted_iota(jnp.int32, (dests, dests), 0) == lax.broadcasted_iota(jnp.int32, (dests, dests), 1)
    counts = jnp.where(eye, counts_ref[...].astype(jnp.float32), 0.0)
    counts = jnp.sum(counts, axis=1, keepdims=True).astype(jnp.int32)
    live = lax.broadcasted_iota(jnp.int32, (dests, cap), 1) < counts
    code = jnp.where(live, cells_ref[...], dead)
    fixed = [
        jnp.minimum((offsets_ref[i] * STEPS + 0.5).astype(jnp.int32), STEPS - 1) for i in range(3)
    ]
    first = fixed[0] | (fixed[2] << BITS)
    second = fixed[1] | ((fixed[2] >> (32 - BITS)) << BITS)
    codes = code[:, : cap // 2] | (code[:, cap // 2 :] << 16)
    for dest in range(dests):
        words_ref[dest, :, 0:cap] = first[dest : dest + 1]
        words_ref[dest, :, cap : 2 * cap] = second[dest : dest + 1]
        words_ref[dest, :, 2 * cap :] = codes[dest : dest + 1]


def packed_slots(cells, offsets, counts, width_x, width_y, depth_z):
    dests, cap = cells.shape
    return pl.pallas_call(
        functools.partial(pack_kernel, 2 * width_x * width_y * depth_z),
        out_shape=jax.ShapeDtypeStruct((dests, 1, 5 * cap // 2), jnp.int32),
        in_specs=[pl.BlockSpec(memory_space=pltpu.HBM)] * 3,
        out_specs=pl.BlockSpec(memory_space=pltpu.VMEM),
        scratch_shapes=[
            pltpu.VMEM((dests, cap), jnp.int32),
            pltpu.VMEM((3, dests, cap), jnp.float32),
            pltpu.VMEM((1, dests), jnp.int32),
            pltpu.SemaphoreType.DMA((3,)),
        ],
        compiler_params=pltpu.CompilerParams(vmem_limit_bytes=60 * 1024 * 1024),
        name="pack",
    )(cells, offsets.transpose(1, 0, 2), counts)


def deposit_kernel(width_x, width_y, depth_z, cap, words_ref, after_ref, late_ref, out_ref, acc_ref):
    rows = out_ref.shape[0]
    acc_ref[...] = jnp.zeros_like(acc_ref)
    slot_rows = cap // 128
    source_rows = slot_rows * 5 // 2
    group = 16 // slot_rows
    row_id = lax.broadcasted_iota(jnp.int32, (8, 128), 0)
    z_id = lax.broadcasted_iota(jnp.int32, (depth_z, 128), 0).astype(jnp.float32).astype(jnp.bfloat16)
    one, zero = jnp.bfloat16(1.0), jnp.bfloat16(0.0)

    def body(i, carry):
        block = words_ref[pl.ds(pl.multiple_of(i * group * source_rows, 8), group * source_rows), :]

        def gathered(start, length):
            parts = [block[k * source_rows + start : k * source_rows + start + length] for k in range(group)]
            return parts

        first = jnp.concatenate(gathered(0, slot_rows), axis=0)
        second = jnp.concatenate(gathered(slot_rows, slot_rows), axis=0)
        halves = gathered(2 * slot_rows, slot_rows // 2)
        code = jnp.concatenate([part for half in halves for part in (half & 0xFFFF, (half >> 16) & 0xFFFF)], axis=0)
        inv = 1.0 / STEPS
        fixed_z = ((first >> BITS) & ((1 << (32 - BITS)) - 1)) | ((second >> BITS) << (32 - BITS))
        frac_x = (first & (STEPS - 1)).astype(jnp.float32) * inv
        frac_y = (second & (STEPS - 1)).astype(jnp.float32) * inv
        frac_z = fixed_z.astype(jnp.float32) * inv
        cell_z = (code % depth_z).astype(jnp.float32)
        column = code // depth_z
        cell_y = column % width_y
        cell_x = column // width_y
        past = jnp.where(cell_y == width_y - 1, frac_y, 0.0)
        rest_x, rest_y, rest_z = 1.0 - frac_x, 1.0 - frac_y, 1.0 - frac_z
        weights, hot = [], []
        for k in range(16):
            row = slice(k, k + 1)
            at_y, at_x = cell_y[row], cell_x[row]
            wy = jnp.where(at_y == row_id, rest_y[row], jnp.where(at_y + 1 == row_id, frac_y[row], 0.0))
            wx = jnp.where(at_x == row_id, rest_x[row], jnp.where(at_x + 1 == row_id, frac_x[row], 0.0))
            parts = [wx[x : x + 1] * wy for x in range(width_x + 1)] + [wx * past[row]]
            area = jnp.concatenate(parts, axis=0)
            low, high = area * rest_z[row], area * frac_z[row]
            low_a, high_a = low.astype(jnp.bfloat16), high.astype(jnp.bfloat16)
            low_b = (low - low_a.astype(jnp.float32)).astype(jnp.bfloat16)
            high_b = (high - high_a.astype(jnp.float32)).astype(jnp.bfloat16)
            weights.append(jnp.concatenate([low_a, low_b, high_a, high_b], axis=0))
            at_z = jnp.broadcast_to(cell_z[row], (depth_z, 128)).astype(jnp.bfloat16)
            hot.append(jnp.where(at_z == z_id, one, zero))
        acc_ref[...] += lax.dot_general(
            jnp.concatenate(weights, axis=1),
            jnp.concatenate(hot, axis=1),
            (((1,), (1,)), ((), ())),
            preferred_element_type=jnp.float32,
        )
        return carry

    lax.fori_loop(0, words_ref.shape[0] // (group * source_rows), body, 0, unroll=16)
    low = acc_ref[0:rows] + acc_ref[rows : 2 * rows]
    high = acc_ref[2 * rows : 3 * rows] + acc_ref[3 * rows : 4 * rows]
    out_ref[...] = low + pltpu.roll(high, 1, axis=1)


def deposit(words, after, late, cap, width_x, width_y, depth_z):
    rows = (width_x + 1) * width_y + 8
    return pl.pallas_call(
        functools.partial(deposit_kernel, width_x, width_y, depth_z, cap),
        out_shape=jax.ShapeDtypeStruct((rows, depth_z), jnp.float32),
        in_specs=[pl.BlockSpec(memory_space=pltpu.VMEM)] * 3,
        out_specs=pl.BlockSpec(memory_space=pltpu.VMEM),
        scratch_shapes=[pltpu.VMEM((4 * rows, depth_z), jnp.float32)],
        compiler_params=pltpu.CompilerParams(vmem_limit_bytes=16 * 1024 * 1024),
        name="deposit",
    )(words.reshape(-1, 128), after, late)


def combine_kernel(width_x, width_y, own_ref, other_ref, near_ref, far_ref):
    full_y = 2 * width_y
    spill = (width_x + 1) * width_y
    top = lax.broadcasted_iota(jnp.int32, (width_y, own_ref.shape[1]), 0) == 0
    planes = []
    for x in range(width_x + 1):
        rows, edge = slice(x * width_y, (x + 1) * width_y), slice(spill + x, spill + x + 1)
        upper = own_ref[rows] + jnp.where(top, other_ref[edge], 0.0)
        lower = other_ref[rows] + jnp.where(top, own_ref[edge], 0.0)
        near_ref[x * full_y : x * full_y + width_y] = upper
        near_ref[x * full_y + width_y : (x + 1) * full_y] = lower
        planes.append((upper, lower))
    upward = lax.axis_index("sub") == 0
    for i, (up, down) in enumerate(((width_x - 1, 0), (width_x, 0))):
        for half in range(2):
            start = i * full_y + half * width_y
            far_ref[start : start + width_y] = jnp.where(upward, planes[up][half], planes[down][half])


def combined(own, other, width_x, width_y):
    depth_z = own.shape[1]
    full_y = 2 * width_y
    return pl.pallas_call(
        functools.partial(combine_kernel, width_x, width_y),
        out_shape=(
            jax.ShapeDtypeStruct(((width_x + 1) * full_y, depth_z), jnp.float32),
            jax.ShapeDtypeStruct((2 * full_y, depth_z), jnp.float32),
        ),
        in_specs=[pl.BlockSpec(memory_space=pltpu.VMEM)] * 2,
        out_specs=(pl.BlockSpec(memory_space=pltpu.VMEM),) * 2,
        compiler_params=pltpu.CompilerParams(vmem_limit_bytes=4 * 1024 * 1024),
        name="combine",
    )(own, other)


CH = 16
RIM = 16


def dot(a, b, dims=((1,), (0,))):
    return lax.dot_general(a, b, (dims, ((), ())), preferred_element_type=jnp.float32)


def iota(shape, axis):
    return lax.broadcasted_iota(jnp.int32, shape, axis)


def weights_kernel(
    full_y, raw_ref, after_ref, mats_ref, wfirst_ref, whead_ref, square, taps_ref
):
    lanes = full_y * CH
    f32, bf16 = jnp.float32, jnp.bfloat16
    slot = iota((CH, 128), 1) // CH

    def turned(x, by):
        return x if by % 128 == 0 else pltpu.roll(x, by % 128, axis=1)

    square[...] = jnp.zeros_like(square)
    for which in range(2):
        square[0:CH, :] = raw_ref[:, which * 512 : (which + 1) * 512].astype(f32)
        flipped = jnp.transpose(square[...])
        for dx in range(3):
            for dz in range(3):
                ahead = back = jnp.zeros((CH, 128), f32)
                for dy in range(3):
                    start = (dx * 9 + dy * 3 + dz) * CH
                    ahead = ahead + turned(flipped[start : start + CH], dy * CH)
                    block = start // 128 * 128
                    picked = jnp.where(slot == (start - block) // CH, square[0:CH, block : block + 128], 0.0)
                    back = back + turned(picked, dy * CH - (start - block))
                rows = slice((dx * 3 + dz) * CH, (dx * 3 + dz + 1) * CH)
                taps_ref[which, rows, :] = ahead.astype(bf16)
                taps_ref[2 + which, rows, :] = back.astype(bf16)

    row, lane = iota((128, lanes), 0), iota((128, lanes), 1)
    same = row % CH == lane % CH
    shift, lane_y = row // CH - 1, lane // CH

    def body(y, carry):
        forward = jnp.where(same & (lane_y == (y - shift + full_y) % full_y), 1.0, 0.0).astype(bf16)
        back = jnp.where(same & (lane_y == (y + shift + full_y) % full_y), 1.0, 0.0).astype(bf16)
        for which in range(4):
            spread = dot(taps_ref[which], forward if which < 2 else back).astype(bf16)
            for dx in range(3):
                for dz in range(3):
                    tap = dx * 3 + dz if which < 2 else (2 - dx) * 3 + 2 - dz
                    start = pl.multiple_of(dz * lanes + y * CH, CH)
                    mats_ref[which, dx, pl.ds(start, CH), :] = spread[tap * CH : (tap + 1) * CH]
        return carry

    lax.fori_loop(0, full_y, body, 0, unroll=4)

    rows = 9 * full_y
    at_y, at_lane = iota((rows, lanes), 0) % full_y, iota((rows, lanes), 1) // CH
    square[...] = jnp.zeros_like(square)
    square[0:CH, 0:128] = raw_ref[:, 1024:1152].astype(f32)
    flipped = jnp.transpose(square[:, 0:128])
    spread_rows = []
    for dx in range(3):
        for dz in range(3):
            line = jnp.zeros((1, 128), f32)
            for dy in range(3):
                tap = dx * 9 + dy * 3 + dz
                line = line + turned(flipped[tap : tap + 1], dy * CH)
            spread_rows.append(jnp.broadcast_to(line, (full_y, 128)))
    first = jnp.concatenate(spread_rows, axis=0).astype(bf16)
    total = jnp.zeros((rows, lanes), f32)
    for dy in range(3):
        pick = jnp.where(same & (row // CH == dy), 1.0, 0.0).astype(bf16)
        total = jnp.where(at_y == (at_lane + dy - 1 + full_y) % full_y, dot(first, pick), total)
    wfirst_ref[...] = total.astype(bf16)

    rows = 3 * full_y
    at_y, at_lane = iota((rows, lanes), 0) % full_y, iota((rows, lanes), 1) // CH
    square[...] = jnp.zeros_like(square)
    square[0:CH, 0:128] = raw_ref[:, 1152:1280].astype(f32)
    head = [jnp.broadcast_to(square[k : k + 1, 0:128], (full_y, 128)) for k in range(3)]
    head = jnp.concatenate(head, axis=0).astype(bf16)
    for half in range(2):
        pick = jnp.where(row == lane % CH + half * CH, 1.0, 0.0).astype(bf16)
        whead_ref[half] = jnp.where(at_y == at_lane, dot(head, pick), 0.0).astype(bf16)


def side_by_side(w_first, w_mid, w_last, w_head):
    def widened(w, columns):
        return jnp.pad(w, ((0, CH - w.shape[0]), (0, columns - w.shape[1])))

    return jnp.concatenate([widened(w_mid, 512), widened(w_last, 512), widened(w_first, 128), widened(w_head, 128)], axis=1)


def weight_matrices(raw, after, full_y):
    lanes = full_y * CH
    return pl.pallas_call(
        functools.partial(weights_kernel, full_y),
        out_shape=(
            jax.ShapeDtypeStruct((4, 3, 3 * lanes, lanes), jnp.bfloat16),
            jax.ShapeDtypeStruct((9 * full_y, lanes), jnp.bfloat16),
            jax.ShapeDtypeStruct((2, 3 * full_y, lanes), jnp.bfloat16),
        ),
        in_specs=[pl.BlockSpec(memory_space=pltpu.VMEM)] * 2,
        out_specs=(pl.BlockSpec(memory_space=pltpu.VMEM),) * 3,
        scratch_shapes=[pltpu.VMEM((128, 512), jnp.float32), pltpu.VMEM((4, 9 * CH, 128), jnp.bfloat16)],
        compiler_params=pltpu.CompilerParams(vmem_limit_bytes=16 * 1024 * 1024),
        cost_estimate=pl.CostEstimate(flops=2 * 4 * 9 * CH * 128 * lanes * full_y, bytes_accessed=8 << 20, transcendentals=0),
        name="weights",
    )(raw, after)


def edges_kernel(width_x, width_y, own_ref, other_ref, middle_ref, edge_ref):
    full_y = 2 * width_y
    upward = lax.axis_index("sub") == 0
    for k in range(3):
        rows = slice(k * full_y, (k + 1) * full_y)
        planes = []
        for x in range(width_x):
            both = [own_ref[k, x].astype(jnp.float32), other_ref[k, x].astype(jnp.float32)]
            planes.append(jnp.concatenate(both, axis=0))
            middle_ref[x, rows] = planes[x].astype(jnp.bfloat16)
        for i in range(2):
            edge_ref[i, rows] = jnp.where(upward, planes[width_x - 2 + i], planes[i]).astype(jnp.bfloat16)


def edges(own, other):
    _, width_x, width_y, depth_z = own.shape
    return pl.pallas_call(
        functools.partial(edges_kernel, width_x, width_y),
        out_shape=(
            jax.ShapeDtypeStruct((width_x, 6 * width_y, depth_z), jnp.bfloat16),
            jax.ShapeDtypeStruct((2, 6 * width_y, depth_z), jnp.bfloat16),
        ),
        in_specs=[pl.BlockSpec(memory_space=pltpu.VMEM)] * 2,
        out_specs=(pl.BlockSpec(memory_space=pltpu.VMEM),) * 2,
        compiler_params=pltpu.CompilerParams(vmem_limit_bytes=4 * 1024 * 1024),
        name="edges",
    )(own, other)


def sigmoid(v):
    return 0.5 + 0.5 * jnp.tanh(0.5 * v)


def chain_kernel(
    width_x,
    width_y,
    near_ref,
    near_mine,
    near_theirs,
    far_mine,
    far_theirs,
    ct_middle,
    ct_mine,
    ct_theirs,
    mats_ref,
    wfirst_ref,
    whead_ref,
    force_mine,
    force_theirs,
    mine_ref,
    theirs_ref,
    ct_ref,
    dens,
    dens_inner,
    one,
    two,
    three,
    g_three,
    g_two,
    pre_one,
    pre_two,
    wg,
):
    full_y = 2 * width_y
    full = ct_middle.shape[2]
    half = full // 2
    depth = half + 2 * RIM
    inner = slice(RIM, RIM + half)
    lanes = full_y * CH
    first_core = lax.axis_index("sub") == 0

    def turned(ref, plane):
        start = plane * full_y
        return jnp.concatenate([ref[start + width_y : start + full_y], ref[start : start + width_y]], axis=0)

    def straight(ref, plane):
        return ref[plane * full_y : (plane + 1) * full_y]

    planes = [straight(near_ref, x) for x in range(width_x + 1)]
    below = [jnp.where(first_core, straight(near_mine, x), turned(near_theirs, x)) for x in range(width_x + 1)]
    above = [jnp.where(first_core, turned(near_theirs, x), straight(near_mine, x)) for x in range(width_x + 1)]
    tail = [jnp.where(first_core, straight(far_mine, x), turned(far_theirs, x)) for x in range(2)]
    ahead = jnp.where(first_core, turned(far_theirs, 0), straight(far_mine, 0))
    column = [tail[0], tail[1] + below[0], *below[1:width_x], below[width_x] + planes[0], *planes[1:width_x]]
    column = column + [planes[width_x] + above[0], *above[1:width_x], above[width_x] + ahead]
    n_dens = 3 * width_x + 2
    def framed(field):
        return jnp.where(first_core, pltpu.roll(field, RIM, axis=1), pltpu.roll(field, half + RIM, axis=1))

    def around(plane):
        return jnp.concatenate([pltpu.roll(plane, 1, axis=1), plane, pltpu.roll(plane, full - 1, axis=1)], axis=0)

    def chosen(field):
        return jnp.where(first_core, field[:, 0:half], field[:, half:full])

    for j in range(n_dens):
        rows = slice(3 * full_y * j, 3 * full_y * (j + 1))
        dens[rows] = around(framed(column[j]))[:, 0:depth].astype(jnp.bfloat16)
        if 0 <= j - 4 < width_x + 2:
            rows = slice(3 * full_y * (j - 4), 3 * full_y * (j - 3))
            dens_inner[rows] = chosen(around(column[j])).astype(jnp.bfloat16)

    ct_inner = []
    for x in range(width_x):
        plane = ct_middle[x].astype(jnp.float32)
        ct_ref[x + 2] = framed(plane)[:, 0:depth].astype(jnp.bfloat16)
        ct_inner.append(chosen(plane).astype(jnp.bfloat16))
    for x in range(2):
        mine, theirs = framed(ct_mine[x].astype(jnp.float32)), framed(ct_theirs[x].astype(jnp.float32))
        halves = [theirs[i * width_y : (i + 1) * width_y] for i in (1, 0, 3, 2, 5, 4)]
        theirs = jnp.concatenate(halves, axis=0)
        ct_ref[x] = jnp.where(first_core, mine, theirs)[:, 0:depth].astype(jnp.bfloat16)
        ct_ref[x + 2 + width_x] = jnp.where(first_core, theirs, mine)[:, 0:depth].astype(jnp.bfloat16)

    def window(x):
        return dens[pl.ds(pl.multiple_of(3 * full_y * x, 3 * full_y), 9 * full_y), :]

    def put(ref, x, field):
        ref[x, :, 0:lanes] = pltpu.roll(field, 1, axis=0).astype(jnp.bfloat16)
        ref[x, :, lanes : 2 * lanes] = field.astype(jnp.bfloat16)
        ref[x, :, 2 * lanes : 3 * lanes] = pltpu.roll(field, depth - 1, axis=0).astype(jnp.bfloat16)

    def conv(ref, x, which):
        total = None
        for dx in range(3):
            part = dot(ref[x + dx : x + dx + 2].reshape(2 * depth, 3 * lanes), mats_ref[which, dx])
            total = part if total is None else total + part
        return total.reshape(2, depth, lanes)

    def slope(v):
        s = sigmoid(v)
        return s * (1.0 + v * (1.0 - s))

    def first_plane(x):
        v = dot(window(x), wfirst_ref[...], ((0,), (0,)))
        if 0 <= x - 4 < width_x:
            pre_one[x - 4] = v
        put(one, x, v * sigmoid(v))

    def second_done(i, both):
        for k in range(2):
            v, x = both[k], 2 * i + k
            if 0 <= x - 2 < width_x + 2:
                pre_two[x - 2] = v
            put(two, x, v * sigmoid(v))

    def third_done(i, both):
        for k in range(2):
            v, x = both[k], 2 * i + k
            s = sigmoid(v)
            if 0 <= x - 2 < width_x:
                three[x - 2] = (v * s).astype(jnp.bfloat16)
            back = dot(ct_ref[x], whead_ref[0], ((0,), (0,)))
            put(g_three, x, back * (s * (1.0 + v * (1.0 - s))))

    def back_done(i, both):
        for k in range(2):
            x = 2 * i + k
            put(g_two, x, both[k] * slope(pre_two[x]))

    layers = ((one, 0, second_done), (two, 1, third_done), (g_three, 3, back_done))
    pairs = [(n_dens - 4 - 2 * layer) // 2 for layer in range(3)]
    order = sorted(
        ((i + 2.6 * layer, layer, i) for layer in range(3) for i in range(pairs[layer])),
    )
    firsts_done = 0
    waiting = None
    for _, layer, i in order:
        if layer == 0:
            while firsts_done < 2 * i + 4:
                first_plane(firsts_done)
                firsts_done += 1
        elif waiting is not None and waiting[0] == layer - 1 and waiting[1] <= i + 1:
            layers[waiting[0]][2](waiting[1], waiting[2])
            waiting = None
        ref, which, done = layers[layer]
        both = conv(ref, 2 * i, which)
        if waiting is not None:
            layers[waiting[0]][2](waiting[1], waiting[2])
        waiting = (layer, i, both)
    layers[waiting[0]][2](waiting[1], waiting[2])

    ct_own = jnp.concatenate(ct_inner, axis=1)
    heads = [
        dot(ct_own, three[:, inner, :].reshape(width_x * half, lanes)),
        dot(ct_own, one[4 : 4 + width_x, inner, lanes : 2 * lanes].reshape(width_x * half, lanes)),
    ]
    for x in range(width_x):
        rows = dot(three[x, inner, :], whead_ref[0], ((1,), (1,)))
        rows = jnp.transpose(rows + dot(one[x + 4, inner, lanes : 2 * lanes], whead_ref[1], ((1,), (1,))))
        for k in range(3):
            start = k * full_y
            force_mine[k, x] = rows[start : start + width_y].astype(jnp.bfloat16)
            force_theirs[k, x] = rows[start + width_y : start + full_y].astype(jnp.bfloat16)

    for which, grads, fields, shift in ((0, g_three, two, (2, 2)), (1, g_two, one, (1, 3))):
        across = [jnp.transpose(grads[x + shift[0], inner, lanes : 2 * lanes]) for x in range(width_x)]
        across = jnp.concatenate(across, axis=1)
        for dx in range(3):
            field = fields[shift[1] + dx : shift[1] + dx + width_x, inner, :]
            wg[which, dx] = dot(across, field.reshape(width_x * half, 3 * lanes))
    grad_one = []
    for i in range(width_x // 2):
        both = conv(g_two, 2 * i, 2)
        for k in range(2):
            x = 2 * i + k
            back = both[k] + dot(ct_ref[x + 2], whead_ref[1], ((0,), (0,)))
            grad_one.append((back * slope(pre_one[x])).astype(jnp.bfloat16)[inner])
    windows = jnp.concatenate(
        [dens_inner[3 * full_y * x : 3 * full_y * (x + 3)] for x in range(width_x)], axis=1
    )
    firsts = dot(windows, jnp.concatenate(grad_one, axis=0))

    lane = iota((CH, 128), 1)

    def gathered(which):
        blocks = [jnp.zeros((CH, 128), jnp.float32) for _ in range(4)]
        for dx in range(3):
            for dz in range(3):
                lined = jnp.zeros((CH, lanes), jnp.float32)
                for y in range(full_y):
                    piece = wg[which, dx, y * CH : (y + 1) * CH, dz * lanes : (dz + 1) * lanes]
                    turn = (lanes - CH * (y - 1)) % lanes
                    lined = lined + (piece if turn == 0 else pltpu.roll(piece, turn, axis=1))
                for dy in range(3):
                    target = (dx * 9 + dy * 3 + dz) * CH
                    turn = (target - dy * CH) % 128
                    piece = jnp.where(lane // CH == dy, lined[:, 0:128], 0.0)
                    blocks[target // 128] += piece if turn == 0 else pltpu.roll(piece, turn, axis=1)
        return blocks

    def folded(rows):
        rows = sum(rows[:, i * 128 : (i + 1) * 128] for i in range(lanes // 128))
        for turn in (64, 32, 16):
            rows = rows + pltpu.roll(rows, turn, axis=1)
        return rows

    last, mid = gathered(0), gathered(1)
    at_y, at_lane = iota((full_y, lanes), 0), iota((full_y, lanes), 1) // CH
    first_rows = []
    for dx in range(3):
        for dy in range(3):
            match = at_y == (at_lane + dy - 1 + full_y) % full_y
            for dz in range(3):
                tap = (dx * 3 + dz) * full_y
                part = jnp.where(match, firsts[tap : tap + full_y, :], 0.0)
                first_rows.append(jnp.sum(part, axis=0, keepdims=True))
    first = folded(jnp.concatenate(first_rows + [jnp.zeros((5, lanes), jnp.float32)], axis=0))
    gap = jnp.zeros((48, 128), jnp.float32)
    last[3] += jnp.transpose(jnp.concatenate([gap, first, gap], axis=0))[0:CH]
    for part_of in range(2):
        rows = []
        for k in range(3):
            part = jnp.where(at_y == at_lane, heads[part_of][k * full_y : (k + 1) * full_y], 0.0)
            rows.append(jnp.sum(part, axis=0, keepdims=True))
        head = folded(jnp.concatenate(rows + [jnp.zeros((CH - 3, lanes), jnp.float32)], axis=0))
        last[3] += jnp.where(lane // CH == 5 + part_of, head, 0.0)
    for block in range(4):
        columns = slice(block * 128, (block + 1) * 128)
        mine_ref[:, columns] = jnp.where(first_core, last[block], mid[block])
        theirs_ref[:, columns] = jnp.where(first_core, mid[block], last[block])


def chain(pieces, mats, wfirst, whead, width_x, width_y, depth_z):
    full_y = 2 * width_y
    lanes = full_y * CH
    half = depth_z // 2
    depth = half + 2 * RIM
    n_dens = 3 * width_x + 2
    bf16, f32 = jnp.bfloat16, jnp.float32
    args = (*pieces, mats, wfirst, whead)
    return pl.pallas_call(
        functools.partial(chain_kernel, width_x, width_y),
        out_shape=(
            jax.ShapeDtypeStruct((3, width_x, width_y, half), bf16),
            jax.ShapeDtypeStruct((3, width_x, width_y, half), bf16),
            jax.ShapeDtypeStruct((CH, 512), f32),
            jax.ShapeDtypeStruct((CH, 512), f32),
        ),
        in_specs=[pl.BlockSpec(memory_space=pltpu.VMEM)] * len(args),
        out_specs=(pl.BlockSpec(memory_space=pltpu.VMEM),) * 4,
        scratch_shapes=[
            pltpu.VMEM((width_x + 4, 3 * full_y, depth), bf16),
            pltpu.VMEM((n_dens * 3 * full_y, depth), bf16),
            pltpu.VMEM(((width_x + 2) * 3 * full_y, half), bf16),
            pltpu.VMEM((n_dens - 2, depth, 3 * lanes), bf16),
            pltpu.VMEM((n_dens - 4, depth, 3 * lanes), bf16),
            pltpu.VMEM((width_x, depth, lanes), bf16),
            pltpu.VMEM((n_dens - 6, depth, 3 * lanes), bf16),
            pltpu.VMEM((n_dens - 8, depth, 3 * lanes), bf16),
            pltpu.VMEM((width_x, depth, lanes), f32),
            pltpu.VMEM((width_x + 2, depth, lanes), f32),
            pltpu.VMEM((2, 3, lanes, 3 * lanes), f32),
        ],
        compiler_params=pltpu.CompilerParams(vmem_limit_bytes=36 * 1024 * 1024),
        name="chain",
    )(*args)


def passed_along(x, axis, by):
    devices = lax.axis_size(axis)
    return lax.ppermute(x, axis, [(i, (i + by) % devices) for i in range(devices)])


def exchanged(x, axis, mask):
    return lax.ppermute(x, axis, [(i, i ^ mask) for i in range(lax.axis_size(axis))])


def summed(mine, theirs):
    total = mine + exchanged(theirs, "sub", 1)
    stride, chips = 1, lax.axis_size("slab")
    while stride < chips:
        if chips // stride >= 4:
            got = [exchanged(total, "slab", stride * i) for i in (1, 2, 3)]
            total = (total + got[0]) + (got[1] + got[2])
            stride *= 4
        else:
            total = total + exchanged(total, "slab", stride)
            stride *= 2
    return total, exchanged(total, "sub", 1)


def finish_kernel(
    loss_scale, mine_ref, theirs_ref, force_mine, force_theirs, force_ref, first_ref, mid_ref, last_ref, head_ref
):
    first_core = lax.axis_index("sub") == 0
    taps = 27 * CH
    mine, theirs = mine_ref[...] * loss_scale, theirs_ref[...] * loss_scale
    mid = jnp.where(first_core, theirs, mine)
    last = jnp.where(first_core, mine, theirs)
    mid_ref[...] = mid[:, :taps]
    last_ref[...] = last[:, :taps]
    half = force_mine.shape[3]
    for k in range(force_ref.shape[0]):
        for x in range(force_ref.shape[1]):
            ours, other = force_mine[k, x].astype(jnp.float32), force_theirs[k, x].astype(jnp.float32)
            force_ref[k, x, :, 0:half] = jnp.where(first_core, ours, other).astype(jnp.bfloat16)
            force_ref[k, x, :, half:] = jnp.where(first_core, other, ours).astype(jnp.bfloat16)
    both = mine[:, 384:] + theirs[:, 384:]
    first_ref[...] = pltpu.roll(both, 80, axis=1)[:, :27]
    head_ref[...] = pltpu.roll(both, 48, axis=1)[:3, : 2 * CH]


def finished(mine, theirs, force_mine, force_theirs, loss_scale):
    f32 = jnp.float32
    _, width_x, width_y, half = force_mine.shape
    return pl.pallas_call(
        functools.partial(finish_kernel, loss_scale),
        out_shape=(
            jax.ShapeDtypeStruct((3, width_x, width_y, 2 * half), jnp.bfloat16),
            jax.ShapeDtypeStruct((CH, 27), f32),
            jax.ShapeDtypeStruct((CH, 27 * CH), f32),
            jax.ShapeDtypeStruct((CH, 27 * CH), f32),
            jax.ShapeDtypeStruct((3, 2 * CH), f32),
        ),
        in_specs=[pl.BlockSpec(memory_space=pltpu.VMEM)] * 4,
        out_specs=(pl.BlockSpec(memory_space=pltpu.VMEM),) * 5,
        compiler_params=pltpu.CompilerParams(vmem_limit_bytes=4 * 1024 * 1024),
        name="finish",
    )(mine, theirs, force_mine, force_theirs)


def per_device(part_cells, part_offsets, part_counts, w_first, w_mid, w_last, w_head, cotangent):
    n_slab = lax.axis_size("slab")
    n_sub = lax.axis_size("sub")
    axes = ("slab", "sub")
    width_x = cotangent.shape[1]
    width_y = cotangent.shape[2]
    depth_z = cotangent.shape[3]
    cap = part_cells.shape[2]

    def outward(x, by):
        pairs = []
        for i in range(n_slab):
            pairs.append((i * n_sub, (i + by) % n_slab * n_sub))
            pairs.append((i * n_sub + 1, (i - by) % n_slab * n_sub + 1))
        return lax.ppermute(x, axes, pairs)

    raw = side_by_side(w_first, w_mid, w_last, w_head)
    words = packed_slots(part_cells[0], part_offsets[0], part_counts, width_x, width_y, depth_z)
    ct_other = exchanged(cotangent, "sub", 1)
    words, ct_other = lax.optimization_barrier((words, ct_other))
    ct_middle, ct_edge = edges(cotangent, ct_other)
    ct_mine = outward(ct_edge, 1)
    ct_theirs = exchanged(ct_mine, "sub", 1)
    got = lax.all_to_all(words, axes, split_axis=0, concat_axis=0, tiled=True)
    own = deposit(got, ct_mine, raw, cap, width_x, width_y, depth_z)
    near, far = combined(own, exchanged(own, "sub", 1), width_x, width_y)
    mats, wfirst, whead = weight_matrices(raw, far, n_sub * width_y)
    near_mine, far_mine, whead = lax.optimization_barrier((outward(near, 1), outward(far, 2), whead))
    near_theirs, far_theirs = exchanged(near_mine, "sub", 1), exchanged(far_mine, "sub", 1)
    pieces = (near, near_mine, near_theirs, far_mine, far_theirs, ct_middle, ct_mine, ct_theirs)
    force_mine, force_theirs, mine, theirs = chain(pieces, mats, wfirst, whead, width_x, width_y, depth_z)
    loss_scale = 1.0 / math.sqrt(width_x * n_slab * width_y * n_sub * depth_z)
    force_theirs = exchanged(force_theirs, "sub", 1)
    return finished(*summed(mine, theirs), force_mine, force_theirs, loss_scale)


def solution(mesh):
    in_specs = (
        P(("slab", "sub"), None, None),
        P(("slab", "sub"), None, None, None),
        P(("slab", "sub"), None),
        P(),
        P(),
        P(),
        P(),
        P(None, "slab", "sub", None),
    )
    out_specs = (P(None, "slab", "sub", None), P(), P(), P(), P())
    return jax.shard_map(
        per_device, mesh=mesh, in_specs=in_specs, out_specs=out_specs, check_vma=False
    )
```

```python
import functools
import math

import jax
import jax.numpy as jnp
from jax import lax
from jax.experimental import pallas as pl
from jax.experimental.pallas import tpu as pltpu
from jax.sharding import PartitionSpec as P

BITS = 21
STEPS = 1 << BITS


def pack_kernel(dead, cells_hbm, offsets_hbm, counts_hbm, words_ref, cells_ref, offsets_ref, counts_ref, sems):
    dests, cap = cells_ref.shape
    copies = [
        pltpu.make_async_copy(source, target, sems.at[i])
        for i, (source, target) in enumerate(
            ((counts_hbm, counts_ref), (cells_hbm, cells_ref), (offsets_hbm, offsets_ref))
        )
    ]
    for copy in copies:
        copy.start()
    for copy in copies:
        copy.wait()
    eye = lax.broadcasted_iota(jnp.int32, (dests, dests), 0) == lax.broadcasted_iota(jnp.int32, (dests, dests), 1)
    counts = jnp.where(eye, counts_ref[...].astype(jnp.float32), 0.0)
    counts = jnp.sum(counts, axis=1, keepdims=True).astype(jnp.int32)
    live = lax.broadcasted_iota(jnp.int32, (dests, cap), 1) < counts
    code = jnp.where(live, cells_ref[...], dead)
    fixed = [
        jnp.minimum((offsets_ref[i] * STEPS + 0.5).astype(jnp.int32), STEPS - 1) for i in range(3)
    ]
    first = fixed[0] | (fixed[2] << BITS)
    second = fixed[1] | ((fixed[2] >> (32 - BITS)) << BITS)
    codes = code[:, : cap // 2] | (code[:, cap // 2 :] << 16)
    for dest in range(dests):
        words_ref[dest, :, 0:cap] = first[dest : dest + 1]
        words_ref[dest, :, cap : 2 * cap] = second[dest : dest + 1]
        words_ref[dest, :, 2 * cap :] = codes[dest : dest + 1]


def packed_slots(cells, offsets, counts, width_x, width_y, depth_z):
    dests, cap = cells.shape
    return pl.pallas_call(
        functools.partial(pack_kernel, 2 * width_x * width_y * depth_z),
        out_shape=jax.ShapeDtypeStruct((dests, 1, 5 * cap // 2), jnp.int32),
        in_specs=[pl.BlockSpec(memory_space=pltpu.HBM)] * 3,
        out_specs=pl.BlockSpec(memory_space=pltpu.VMEM),
        scratch_shapes=[
            pltpu.VMEM((dests, cap), jnp.int32),
            pltpu.VMEM((3, dests, cap), jnp.float32),
            pltpu.VMEM((1, dests), jnp.int32),
            pltpu.SemaphoreType.DMA((3,)),
        ],
        compiler_params=pltpu.CompilerParams(vmem_limit_bytes=60 * 1024 * 1024),
        name="pack",
    )(cells, offsets.transpose(1, 0, 2), counts)


def deposit_kernel(width_x, width_y, depth_z, cap, words_ref, after_ref, late_ref, out_ref, acc_ref):
    rows = out_ref.shape[0]
    acc_ref[...] = jnp.zeros_like(acc_ref)
    slot_rows = cap // 128
    source_rows = slot_rows * 5 // 2
    group = 16 // slot_rows
    row_id = lax.broadcasted_iota(jnp.int32, (8, 128), 0)
    z_id = lax.broadcasted_iota(jnp.int32, (depth_z, 128), 0).astype(jnp.float32).astype(jnp.bfloat16)
    one, zero = jnp.bfloat16(1.0), jnp.bfloat16(0.0)

    def body(i, carry):
        block = words_ref[pl.ds(pl.multiple_of(i * group * source_rows, 8), group * source_rows), :]

        def gathered(start, length):
            parts = [block[k * source_rows + start : k * source_rows + start + length] for k in range(group)]
            return parts

        first = jnp.concatenate(gathered(0, slot_rows), axis=0)
        second = jnp.concatenate(gathered(slot_rows, slot_rows), axis=0)
        halves = gathered(2 * slot_rows, slot_rows // 2)
        code = jnp.concatenate([part for half in halves for part in (half & 0xFFFF, (half >> 16) & 0xFFFF)], axis=0)
        inv = 1.0 / STEPS
        fixed_z = ((first >> BITS) & ((1 << (32 - BITS)) - 1)) | ((second >> BITS) << (32 - BITS))
        frac_x = (first & (STEPS - 1)).astype(jnp.float32) * inv
        frac_y = (second & (STEPS - 1)).astype(jnp.float32) * inv
        frac_z = fixed_z.astype(jnp.float32) * inv
        cell_z = (code % depth_z).astype(jnp.float32)
        column = code // depth_z
        cell_y = column % width_y
        cell_x = column // width_y
        past = jnp.where(cell_y == width_y - 1, frac_y, 0.0)
        rest_x, rest_y, rest_z = 1.0 - frac_x, 1.0 - frac_y, 1.0 - frac_z
        weights, hot = [], []
        for k in range(16):
            row = slice(k, k + 1)
            at_y, at_x = cell_y[row], cell_x[row]
            wy = jnp.where(at_y == row_id, rest_y[row], jnp.where(at_y + 1 == row_id, frac_y[row], 0.0))
            wx = jnp.where(at_x == row_id, rest_x[row], jnp.where(at_x + 1 == row_id, frac_x[row], 0.0))
            parts = [wx[x : x + 1] * wy for x in range(width_x + 1)] + [wx * past[row]]
            area = jnp.concatenate(parts, axis=0)
            low, high = area * rest_z[row], area * frac_z[row]
            low_a, high_a = low.astype(jnp.bfloat16), high.astype(jnp.bfloat16)
            low_b = (low - low_a.astype(jnp.float32)).astype(jnp.bfloat16)
            high_b = (high - high_a.astype(jnp.float32)).astype(jnp.bfloat16)
            weights.append(jnp.concatenate([low_a, low_b, high_a, high_b], axis=0))
            at_z = jnp.broadcast_to(cell_z[row], (depth_z, 128)).astype(jnp.bfloat16)
            hot.append(jnp.where(at_z == z_id, one, zero))
        acc_ref[...] += lax.dot_general(
            jnp.concatenate(weights, axis=1),
            jnp.concatenate(hot, axis=1),
            (((1,), (1,)), ((), ())),
            preferred_element_type=jnp.float32,
        )
        return carry

    lax.fori_loop(0, words_ref.shape[0] // (group * source_rows), body, 0, unroll=16)
    low = acc_ref[0:rows] + acc_ref[rows : 2 * rows]
    high = acc_ref[2 * rows : 3 * rows] + acc_ref[3 * rows : 4 * rows]
    out_ref[...] = low + pltpu.roll(high, 1, axis=1)


def deposit(words, after, late, cap, width_x, width_y, depth_z):
    rows = (width_x + 1) * width_y + 8
    return pl.pallas_call(
        functools.partial(deposit_kernel, width_x, width_y, depth_z, cap),
        out_shape=jax.ShapeDtypeStruct((rows, depth_z), jnp.float32),
        in_specs=[pl.BlockSpec(memory_space=pltpu.VMEM)] * 3,
        out_specs=pl.BlockSpec(memory_space=pltpu.VMEM),
        scratch_shapes=[pltpu.VMEM((4 * rows, depth_z), jnp.float32)],
        compiler_params=pltpu.CompilerParams(vmem_limit_bytes=16 * 1024 * 1024),
        name="deposit",
    )(words.reshape(-1, 128), after, late)


def combine_kernel(width_x, width_y, own_ref, other_ref, near_ref, far_ref):
    full_y = 2 * width_y
    spill = (width_x + 1) * width_y
    top = lax.broadcasted_iota(jnp.int32, (width_y, own_ref.shape[1]), 0) == 0
    planes = []
    for x in range(width_x + 1):
        rows, edge = slice(x * width_y, (x + 1) * width_y), slice(spill + x, spill + x + 1)
        upper = own_ref[rows] + jnp.where(top, other_ref[edge], 0.0)
        lower = other_ref[rows] + jnp.where(top, own_ref[edge], 0.0)
        near_ref[x * full_y : x * full_y + width_y] = upper
        near_ref[x * full_y + width_y : (x + 1) * full_y] = lower
        planes.append((upper, lower))
    upward = lax.axis_index("sub") == 0
    for i, (up, down) in enumerate(((width_x - 1, 0), (width_x, 0))):
        for half in range(2):
            start = i * full_y + half * width_y
            far_ref[start : start + width_y] = jnp.where(upward, planes[up][half], planes[down][half])


def combined(own, other, width_x, width_y):
    depth_z = own.shape[1]
    full_y = 2 * width_y
    return pl.pallas_call(
        functools.partial(combine_kernel, width_x, width_y),
        out_shape=(
            jax.ShapeDtypeStruct(((width_x + 1) * full_y, depth_z), jnp.float32),
            jax.ShapeDtypeStruct((2 * full_y, depth_z), jnp.float32),
        ),
        in_specs=[pl.BlockSpec(memory_space=pltpu.VMEM)] * 2,
        out_specs=(pl.BlockSpec(memory_space=pltpu.VMEM),) * 2,
        compiler_params=pltpu.CompilerParams(vmem_limit_bytes=4 * 1024 * 1024),
        name="combine",
    )(own, other)


CH = 16
RIM = 16


def dot(a, b, dims=((1,), (0,))):
    return lax.dot_general(a, b, (dims, ((), ())), preferred_element_type=jnp.float32)


def iota(shape, axis):
    return lax.broadcasted_iota(jnp.int32, shape, axis)


def weights_kernel(
    full_y, raw_ref, after_ref, mats_ref, wfirst_ref, whead_ref, square, taps_ref
):
    lanes = full_y * CH
    f32, bf16 = jnp.float32, jnp.bfloat16
    slot = iota((CH, 128), 1) // CH

    def turned(x, by):
        return x if by % 128 == 0 else pltpu.roll(x, by % 128, axis=1)

    square[...] = jnp.zeros_like(square)
    for which in range(2):
        square[0:CH, :] = raw_ref[:, which * 512 : (which + 1) * 512].astype(f32)
        flipped = jnp.transpose(square[...])
        for dx in range(3):
            for dz in range(3):
                ahead = back = jnp.zeros((CH, 128), f32)
                for dy in range(3):
                    start = (dx * 9 + dy * 3 + dz) * CH
                    ahead = ahead + turned(flipped[start : start + CH], dy * CH)
                    block = start // 128 * 128
                    picked = jnp.where(slot == (start - block) // CH, square[0:CH, block : block + 128], 0.0)
                    back = back + turned(picked, dy * CH - (start - block))
                rows = slice((dx * 3 + dz) * CH, (dx * 3 + dz + 1) * CH)
                taps_ref[which, rows, :] = ahead.astype(bf16)
                taps_ref[2 + which, rows, :] = back.astype(bf16)

    row, lane = iota((128, lanes), 0), iota((128, lanes), 1)
    same = row % CH == lane % CH
    shift, lane_y = row // CH - 1, lane // CH

    def body(y, carry):
        forward = jnp.where(same & (lane_y == (y - shift + full_y) % full_y), 1.0, 0.0).astype(bf16)
        back = jnp.where(same & (lane_y == (y + shift + full_y) % full_y), 1.0, 0.0).astype(bf16)
        for which in range(4):
            spread = dot(taps_ref[which], forward if which < 2 else back).astype(bf16)
            for dx in range(3):
                for dz in range(3):
                    tap = dx * 3 + dz if which < 2 else (2 - dx) * 3 + 2 - dz
                    start = pl.multiple_of(dz * lanes + y * CH, CH)
                    mats_ref[which, dx, pl.ds(start, CH), :] = spread[tap * CH : (tap + 1) * CH]
        return carry

    lax.fori_loop(0, full_y, body, 0, unroll=4)

    rows = 9 * full_y
    at_y, at_lane = iota((rows, lanes), 0) % full_y, iota((rows, lanes), 1) // CH
    square[...] = jnp.zeros_like(square)
    square[0:CH, 0:128] = raw_ref[:, 1024:1152].astype(f32)
    flipped = jnp.transpose(square[:, 0:128])
    spread_rows = []
    for dx in range(3):
        for dz in range(3):
            line = jnp.zeros((1, 128), f32)
            for dy in range(3):
                tap = dx * 9 + dy * 3 + dz
                line = line + turned(flipped[tap : tap + 1], dy * CH)
            spread_rows.append(jnp.broadcast_to(line, (full_y, 128)))
    first = jnp.concatenate(spread_rows, axis=0).astype(bf16)
    total = jnp.zeros((rows, lanes), f32)
    for dy in range(3):
        pick = jnp.where(same & (row // CH == dy), 1.0, 0.0).astype(bf16)
        total = jnp.where(at_y == (at_lane + dy - 1 + full_y) % full_y, dot(first, pick), total)
    wfirst_ref[...] = total.astype(bf16)

    rows = 3 * full_y
    at_y, at_lane = iota((rows, lanes), 0) % full_y, iota((rows, lanes), 1) // CH
    square[...] = jnp.zeros_like(square)
    square[0:CH, 0:128] = raw_ref[:, 1152:1280].astype(f32)
    head = [jnp.broadcast_to(square[k : k + 1, 0:128], (full_y, 128)) for k in range(3)]
    head = jnp.concatenate(head, axis=0).astype(bf16)
    for half in range(2):
        pick = jnp.where(row == lane % CH + half * CH, 1.0, 0.0).astype(bf16)
        whead_ref[half] = jnp.where(at_y == at_lane, dot(head, pick), 0.0).astype(bf16)


def side_by_side(w_first, w_mid, w_last, w_head):
    def widened(w, columns):
        return jnp.pad(w, ((0, CH - w.shape[0]), (0, columns - w.shape[1])))

    return jnp.concatenate([widened(w_mid, 512), widened(w_last, 512), widened(w_first, 128), widened(w_head, 128)], axis=1)


def weight_matrices(raw, after, full_y):
    lanes = full_y * CH
    return pl.pallas_call(
        functools.partial(weights_kernel, full_y),
        out_shape=(
            jax.ShapeDtypeStruct((4, 3, 3 * lanes, lanes), jnp.bfloat16),
            jax.ShapeDtypeStruct((9 * full_y, lanes), jnp.bfloat16),
            jax.ShapeDtypeStruct((2, 3 * full_y, lanes), jnp.bfloat16),
        ),
        in_specs=[pl.BlockSpec(memory_space=pltpu.VMEM)] * 2,
        out_specs=(pl.BlockSpec(memory_space=pltpu.VMEM),) * 3,
        scratch_shapes=[pltpu.VMEM((128, 512), jnp.float32), pltpu.VMEM((4, 9 * CH, 128), jnp.bfloat16)],
        compiler_params=pltpu.CompilerParams(vmem_limit_bytes=16 * 1024 * 1024),
        cost_estimate=pl.CostEstimate(flops=2 * 4 * 9 * CH * 128 * lanes * full_y, bytes_accessed=8 << 20, transcendentals=0),
        name="weights",
    )(raw, after)


def edges_kernel(width_x, width_y, own_ref, other_ref, middle_ref, edge_ref):
    full_y = 2 * width_y
    upward = lax.axis_index("sub") == 0
    for k in range(3):
        rows = slice(k * full_y, (k + 1) * full_y)
        planes = []
        for x in range(width_x):
            both = [own_ref[k, x].astype(jnp.float32), other_ref[k, x].astype(jnp.float32)]
            planes.append(jnp.concatenate(both, axis=0))
            middle_ref[x, rows] = planes[x].astype(jnp.bfloat16)
        for i in range(2):
            edge_ref[i, rows] = jnp.where(upward, planes[width_x - 2 + i], planes[i]).astype(jnp.bfloat16)


def edges(own, other):
    _, width_x, width_y, depth_z = own.shape
    return pl.pallas_call(
        functools.partial(edges_kernel, width_x, width_y),
        out_shape=(
            jax.ShapeDtypeStruct((width_x, 6 * width_y, depth_z), jnp.bfloat16),
            jax.ShapeDtypeStruct((2, 6 * width_y, depth_z), jnp.bfloat16),
        ),
        in_specs=[pl.BlockSpec(memory_space=pltpu.VMEM)] * 2,
        out_specs=(pl.BlockSpec(memory_space=pltpu.VMEM),) * 2,
        compiler_params=pltpu.CompilerParams(vmem_limit_bytes=4 * 1024 * 1024),
        name="edges",
    )(own, other)


def sigmoid(v):
    return 0.5 + 0.5 * jnp.tanh(0.5 * v)


def chain_kernel(
    width_x,
    width_y,
    near_ref,
    near_mine,
    near_theirs,
    far_mine,
    far_theirs,
    ct_middle,
    ct_mine,
    ct_theirs,
    mats_ref,
    wfirst_ref,
    whead_ref,
    force_mine,
    force_theirs,
    mine_ref,
    theirs_ref,
    ct_ref,
    dens,
    dens_inner,
    one,
    two,
    three,
    g_three,
    g_two,
    pre_one,
    pre_two,
    wg,
):
    full_y = 2 * width_y
    full = ct_middle.shape[2]
    half = full // 2
    depth = half + 2 * RIM
    inner = slice(RIM, RIM + half)
    lanes = full_y * CH
    first_core = lax.axis_index("sub") == 0

    def turned(ref, plane):
        start = plane * full_y
        return jnp.concatenate([ref[start + width_y : start + full_y], ref[start : start + width_y]], axis=0)

    def straight(ref, plane):
        return ref[plane * full_y : (plane + 1) * full_y]

    planes = [straight(near_ref, x) for x in range(width_x + 1)]
    below = [jnp.where(first_core, straight(near_mine, x), turned(near_theirs, x)) for x in range(width_x + 1)]
    above = [jnp.where(first_core, turned(near_theirs, x), straight(near_mine, x)) for x in range(width_x + 1)]
    tail = [jnp.where(first_core, straight(far_mine, x), turned(far_theirs, x)) for x in range(2)]
    ahead = jnp.where(first_core, turned(far_theirs, 0), straight(far_mine, 0))
    column = [tail[0], tail[1] + below[0], *below[1:width_x], below[width_x] + planes[0], *planes[1:width_x]]
    column = column + [planes[width_x] + above[0], *above[1:width_x], above[width_x] + ahead]
    n_dens = 3 * width_x + 2
    def framed(field):
        return jnp.where(first_core, pltpu.roll(field, RIM, axis=1), pltpu.roll(field, half + RIM, axis=1))

    def around(plane):
        return jnp.concatenate([pltpu.roll(plane, 1, axis=1), plane, pltpu.roll(plane, full - 1, axis=1)], axis=0)

    def chosen(field):
        return jnp.where(first_core, field[:, 0:half], field[:, half:full])

    for j in range(n_dens):
        rows = slice(3 * full_y * j, 3 * full_y * (j + 1))
        dens[rows] = around(framed(column[j]))[:, 0:depth].astype(jnp.bfloat16)
        if 0 <= j - 4 < width_x + 2:
            rows = slice(3 * full_y * (j - 4), 3 * full_y * (j - 3))
            dens_inner[rows] = chosen(around(column[j])).astype(jnp.bfloat16)

    ct_inner = []
    for x in range(width_x):
        plane = ct_middle[x].astype(jnp.float32)
        ct_ref[x + 2] = framed(plane)[:, 0:depth].astype(jnp.bfloat16)
        ct_inner.append(chosen(plane).astype(jnp.bfloat16))
    for x in range(2):
        mine, theirs = framed(ct_mine[x].astype(jnp.float32)), framed(ct_theirs[x].astype(jnp.float32))
        halves = [theirs[i * width_y : (i + 1) * width_y] for i in (1, 0, 3, 2, 5, 4)]
        theirs = jnp.concatenate(halves, axis=0)
        ct_ref[x] = jnp.where(first_core, mine, theirs)[:, 0:depth].astype(jnp.bfloat16)
        ct_ref[x + 2 + width_x] = jnp.where(first_core, theirs, mine)[:, 0:depth].astype(jnp.bfloat16)

    def window(x):
        return dens[pl.ds(pl.multiple_of(3 * full_y * x, 3 * full_y), 9 * full_y), :]

    def put(ref, x, field):
        ref[x, :, 0:lanes] = pltpu.roll(field, 1, axis=0).astype(jnp.bfloat16)
        ref[x, :, lanes : 2 * lanes] = field.astype(jnp.bfloat16)
        ref[x, :, 2 * lanes : 3 * lanes] = pltpu.roll(field, depth - 1, axis=0).astype(jnp.bfloat16)

    def conv(ref, x, which):
        total = None
        for dx in range(3):
            part = dot(ref[x + dx : x + dx + 2].reshape(2 * depth, 3 * lanes), mats_ref[which, dx])
            total = part if total is None else total + part
        return total.reshape(2, depth, lanes)

    def slope(v):
        s = sigmoid(v)
        return s * (1.0 + v * (1.0 - s))

    def first_plane(x):
        v = dot(window(x), wfirst_ref[...], ((0,), (0,)))
        if 0 <= x - 4 < width_x:
            pre_one[x - 4] = v
        put(one, x, v * sigmoid(v))

    def second_done(i, both):
        for k in range(2):
            v, x = both[k], 2 * i + k
            if 0 <= x - 2 < width_x + 2:
                pre_two[x - 2] = v
            put(two, x, v * sigmoid(v))

    def third_done(i, both):
        for k in range(2):
            v, x = both[k], 2 * i + k
            s = sigmoid(v)
            if 0 <= x - 2 < width_x:
                three[x - 2] = (v * s).astype(jnp.bfloat16)
            back = dot(ct_ref[x], whead_ref[0], ((0,), (0,)))
            put(g_three, x, back * (s * (1.0 + v * (1.0 - s))))

    def back_done(i, both):
        for k in range(2):
            x = 2 * i + k
            put(g_two, x, both[k] * slope(pre_two[x]))

    layers = ((one, 0, second_done), (two, 1, third_done), (g_three, 3, back_done))
    pairs = [(n_dens - 4 - 2 * layer) // 2 for layer in range(3)]
    order = sorted(
        ((i + 2.6 * layer, layer, i) for layer in range(3) for i in range(pairs[layer])),
    )
    firsts_done = 0
    waiting = None
    for _, layer, i in order:
        if layer == 0:
            while firsts_done < 2 * i + 4:
                first_plane(firsts_done)
                firsts_done += 1
        elif waiting is not None and waiting[0] == layer - 1 and waiting[1] <= i + 1:
            layers[waiting[0]][2](waiting[1], waiting[2])
            waiting = None
        ref, which, done = layers[layer]
        both = conv(ref, 2 * i, which)
        if waiting is not None:
            layers[waiting[0]][2](waiting[1], waiting[2])
        waiting = (layer, i, both)
    layers[waiting[0]][2](waiting[1], waiting[2])

    ct_own = jnp.concatenate(ct_inner, axis=1)
    heads = [
        dot(ct_own, three[:, inner, :].reshape(width_x * half, lanes)),
        dot(ct_own, one[4 : 4 + width_x, inner, lanes : 2 * lanes].reshape(width_x * half, lanes)),
    ]
    for x in range(width_x):
        rows = dot(three[x, inner, :], whead_ref[0], ((1,), (1,)))
        rows = jnp.transpose(rows + dot(one[x + 4, inner, lanes : 2 * lanes], whead_ref[1], ((1,), (1,))))
        for k in range(3):
            start = k * full_y
            force_mine[k, x] = rows[start : start + width_y].astype(jnp.bfloat16)
            force_theirs[k, x] = rows[start + width_y : start + full_y].astype(jnp.bfloat16)

    for which, grads, fields, shift in ((0, g_three, two, (2, 2)), (1, g_two, one, (1, 3))):
        across = [jnp.transpose(grads[x + shift[0], inner, lanes : 2 * lanes]) for x in range(width_x)]
        across = jnp.concatenate(across, axis=1)
        for dx in range(3):
            field = fields[shift[1] + dx : shift[1] + dx + width_x, inner, :]
            wg[which, dx] = dot(across, field.reshape(width_x * half, 3 * lanes))
    grad_one = []
    for i in range(width_x // 2):
        both = conv(g_two, 2 * i, 2)
        for k in range(2):
            x = 2 * i + k
            back = both[k] + dot(ct_ref[x + 2], whead_ref[1], ((0,), (0,)))
            grad_one.append((back * slope(pre_one[x])).astype(jnp.bfloat16)[inner])
    windows = jnp.concatenate(
        [dens_inner[3 * full_y * x : 3 * full_y * (x + 3)] for x in range(width_x)], axis=1
    )
    firsts = dot(windows, jnp.concatenate(grad_one, axis=0))

    lane = iota((CH, 128), 1)

    def gathered(which):
        blocks = [jnp.zeros((CH, 128), jnp.float32) for _ in range(4)]
        for dx in range(3):
            for dz in range(3):
                lined = jnp.zeros((CH, lanes), jnp.float32)
                for y in range(full_y):
                    piece = wg[which, dx, y * CH : (y + 1) * CH, dz * lanes : (dz + 1) * lanes]
                    turn = (lanes - CH * (y - 1)) % lanes
                    lined = lined + (piece if turn == 0 else pltpu.roll(piece, turn, axis=1))
                for dy in range(3):
                    target = (dx * 9 + dy * 3 + dz) * CH
                    turn = (target - dy * CH) % 128
                    piece = jnp.where(lane // CH == dy, lined[:, 0:128], 0.0)
                    blocks[target // 128] += piece if turn == 0 else pltpu.roll(piece, turn, axis=1)
        return blocks

    def folded(rows):
        rows = sum(rows[:, i * 128 : (i + 1) * 128] for i in range(lanes // 128))
        for turn in (64, 32, 16):
            rows = rows + pltpu.roll(rows, turn, axis=1)
        return rows

    last, mid = gathered(0), gathered(1)
    at_y, at_lane = iota((full_y, lanes), 0), iota((full_y, lanes), 1) // CH
    first_rows = []
    for dx in range(3):
        for dy in range(3):
            match = at_y == (at_lane + dy - 1 + full_y) % full_y
            for dz in range(3):
                tap = (dx * 3 + dz) * full_y
                part = jnp.where(match, firsts[tap : tap + full_y, :], 0.0)
                first_rows.append(jnp.sum(part, axis=0, keepdims=True))
    first = folded(jnp.concatenate(first_rows + [jnp.zeros((5, lanes), jnp.float32)], axis=0))
    gap = jnp.zeros((48, 128), jnp.float32)
    last[3] += jnp.transpose(jnp.concatenate([gap, first, gap], axis=0))[0:CH]
    for part_of in range(2):
        rows = []
        for k in range(3):
            part = jnp.where(at_y == at_lane, heads[part_of][k * full_y : (k + 1) * full_y], 0.0)
            rows.append(jnp.sum(part, axis=0, keepdims=True))
        head = folded(jnp.concatenate(rows + [jnp.zeros((CH - 3, lanes), jnp.float32)], axis=0))
        last[3] += jnp.where(lane // CH == 5 + part_of, head, 0.0)
    for block in range(4):
        columns = slice(block * 128, (block + 1) * 128)
        mine_ref[:, columns] = jnp.where(first_core, last[block], mid[block])
        theirs_ref[:, columns] = jnp.where(first_core, mid[block], last[block])


def chain(pieces, mats, wfirst, whead, width_x, width_y, depth_z):
    full_y = 2 * width_y
    lanes = full_y * CH
    half = depth_z // 2
    depth = half + 2 * RIM
    n_dens = 3 * width_x + 2
    bf16, f32 = jnp.bfloat16, jnp.float32
    args = (*pieces, mats, wfirst, whead)
    return pl.pallas_call(
        functools.partial(chain_kernel, width_x, width_y),
        out_shape=(
            jax.ShapeDtypeStruct((3, width_x, width_y, half), bf16),
            jax.ShapeDtypeStruct((3, width_x, width_y, half), bf16),
            jax.ShapeDtypeStruct((CH, 512), f32),
            jax.ShapeDtypeStruct((CH, 512), f32),
        ),
        in_specs=[pl.BlockSpec(memory_space=pltpu.VMEM)] * len(args),
        out_specs=(pl.BlockSpec(memory_space=pltpu.VMEM),) * 4,
        scratch_shapes=[
            pltpu.VMEM((width_x + 4, 3 * full_y, depth), bf16),
            pltpu.VMEM((n_dens * 3 * full_y, depth), bf16),
            pltpu.VMEM(((width_x + 2) * 3 * full_y, half), bf16),
            pltpu.VMEM((n_dens - 2, depth, 3 * lanes), bf16),
            pltpu.VMEM((n_dens - 4, depth, 3 * lanes), bf16),
            pltpu.VMEM((width_x, depth, lanes), bf16),
            pltpu.VMEM((n_dens - 6, depth, 3 * lanes), bf16),
            pltpu.VMEM((n_dens - 8, depth, 3 * lanes), bf16),
            pltpu.VMEM((width_x, depth, lanes), f32),
            pltpu.VMEM((width_x + 2, depth, lanes), f32),
            pltpu.VMEM((2, 3, lanes, 3 * lanes), f32),
        ],
        compiler_params=pltpu.CompilerParams(vmem_limit_bytes=36 * 1024 * 1024),
        name="chain",
    )(*args)


def passed_along(x, axis, by):
    devices = lax.axis_size(axis)
    return lax.ppermute(x, axis, [(i, (i + by) % devices) for i in range(devices)])


def exchanged(x, axis, mask):
    return lax.ppermute(x, axis, [(i, i ^ mask) for i in range(lax.axis_size(axis))])


def summed(mine, theirs, beside):
    total = mine + exchanged(theirs, "sub", 1)
    stride, chips = 1, lax.axis_size("slab")
    while stride < chips:
        if chips // stride >= 4:
            got = [exchanged(total, "slab", stride * i) for i in (1, 2, 3)]
            total = (total + got[0]) + (got[1] + got[2])
            if stride == 1:
                total, beside = lax.optimization_barrier((total, beside))
            stride *= 4
        else:
            total = total + exchanged(total, "slab", stride)
            stride *= 2
    return total, exchanged(total, "sub", 1), beside


def finish_kernel(
    loss_scale, mine_ref, theirs_ref, force_mine, force_theirs, force_ref, first_ref, mid_ref, last_ref, head_ref
):
    first_core = lax.axis_index("sub") == 0
    taps = 27 * CH
    mine, theirs = mine_ref[...] * loss_scale, theirs_ref[...] * loss_scale
    mid = jnp.where(first_core, theirs, mine)
    last = jnp.where(first_core, mine, theirs)
    mid_ref[...] = mid[:, :taps]
    last_ref[...] = last[:, :taps]
    half = force_mine.shape[3]
    for k in range(force_ref.shape[0]):
        for x in range(force_ref.shape[1]):
            ours, other = force_mine[k, x].astype(jnp.float32), force_theirs[k, x].astype(jnp.float32)
            force_ref[k, x, :, 0:half] = jnp.where(first_core, ours, other).astype(jnp.bfloat16)
            force_ref[k, x, :, half:] = jnp.where(first_core, other, ours).astype(jnp.bfloat16)
    both = mine[:, 384:] + theirs[:, 384:]
    first_ref[...] = pltpu.roll(both, 80, axis=1)[:, :27]
    head_ref[...] = pltpu.roll(both, 48, axis=1)[:3, : 2 * CH]


def finished(mine, theirs, force_mine, force_theirs, loss_scale):
    f32 = jnp.float32
    _, width_x, width_y, half = force_mine.shape
    return pl.pallas_call(
        functools.partial(finish_kernel, loss_scale),
        out_shape=(
            jax.ShapeDtypeStruct((3, width_x, width_y, 2 * half), jnp.bfloat16),
            jax.ShapeDtypeStruct((CH, 27), f32),
            jax.ShapeDtypeStruct((CH, 27 * CH), f32),
            jax.ShapeDtypeStruct((CH, 27 * CH), f32),
            jax.ShapeDtypeStruct((3, 2 * CH), f32),
        ),
        in_specs=[pl.BlockSpec(memory_space=pltpu.VMEM)] * 4,
        out_specs=(pl.BlockSpec(memory_space=pltpu.VMEM),) * 5,
        compiler_params=pltpu.CompilerParams(vmem_limit_bytes=4 * 1024 * 1024),
        name="finish",
    )(mine, theirs, force_mine, force_theirs)


def per_device(part_cells, part_offsets, part_counts, w_first, w_mid, w_last, w_head, cotangent):
    n_slab = lax.axis_size("slab")
    n_sub = lax.axis_size("sub")
    axes = ("slab", "sub")
    width_x = cotangent.shape[1]
    width_y = cotangent.shape[2]
    depth_z = cotangent.shape[3]
    cap = part_cells.shape[2]

    def outward(x, by):
        pairs = []
        for i in range(n_slab):
            pairs.append((i * n_sub, (i + by) % n_slab * n_sub))
            pairs.append((i * n_sub + 1, (i - by) % n_slab * n_sub + 1))
        return lax.ppermute(x, axes, pairs)

    raw = side_by_side(w_first, w_mid, w_last, w_head)
    words = packed_slots(part_cells[0], part_offsets[0], part_counts, width_x, width_y, depth_z)
    ct_other = exchanged(cotangent, "sub", 1)
    words, ct_other = lax.optimization_barrier((words, ct_other))
    ct_middle, ct_edge = edges(cotangent, ct_other)
    ct_mine = outward(ct_edge, 1)
    ct_theirs = exchanged(ct_mine, "sub", 1)
    got = lax.all_to_all(words, axes, split_axis=0, concat_axis=0, tiled=True)
    own = deposit(got, ct_mine, raw, cap, width_x, width_y, depth_z)
    near, far = combined(own, exchanged(own, "sub", 1), width_x, width_y)
    mats, wfirst, whead = weight_matrices(raw, far, n_sub * width_y)
    near_mine, far_mine, whead = lax.optimization_barrier((outward(near, 1), outward(far, 2), whead))
    near_theirs, far_theirs = exchanged(near_mine, "sub", 1), exchanged(far_mine, "sub", 1)
    pieces = (near, near_mine, near_theirs, far_mine, far_theirs, ct_middle, ct_mine, ct_theirs)
    force_mine, force_theirs, mine, theirs = chain(pieces, mats, wfirst, whead, width_x, width_y, depth_z)
    loss_scale = 1.0 / math.sqrt(width_x * n_slab * width_y * n_sub * depth_z)
    force_theirs = exchanged(force_theirs, "sub", 1)
    mine, theirs, force_theirs = summed(mine, theirs, force_theirs)
    return finished(mine, theirs, force_mine, force_theirs, loss_scale)


def solution(mesh):
    in_specs = (
        P(("slab", "sub"), None, None),
        P(("slab", "sub"), None, None, None),
        P(("slab", "sub"), None),
        P(),
        P(),
        P(),
        P(),
        P(None, "slab", "sub", None),
    )
    out_specs = (P(None, "slab", "sub", None), P(), P(), P(), P())
    return jax.shard_map(
        per_device, mesh=mesh, in_specs=in_specs, out_specs=out_specs, check_vma=False
    )
```

```python
import functools
import math

import jax
import jax.numpy as jnp
from jax import lax
from jax.experimental import pallas as pl
from jax.experimental.pallas import tpu as pltpu
from jax.sharding import PartitionSpec as P

BITS = 21
STEPS = 1 << BITS


def pack_kernel(dead, cells_hbm, offsets_hbm, counts_hbm, words_ref, cells_ref, offsets_ref, counts_ref, sems):
    dests, cap = cells_ref.shape
    copies = [
        pltpu.make_async_copy(source, target, sems.at[i])
        for i, (source, target) in enumerate(
            ((counts_hbm, counts_ref), (cells_hbm, cells_ref), (offsets_hbm, offsets_ref))
        )
    ]
    for copy in copies:
        copy.start()
    for copy in copies:
        copy.wait()
    eye = lax.broadcasted_iota(jnp.int32, (dests, dests), 0) == lax.broadcasted_iota(jnp.int32, (dests, dests), 1)
    counts = jnp.where(eye, counts_ref[...].astype(jnp.float32), 0.0)
    counts = jnp.sum(counts, axis=1, keepdims=True).astype(jnp.int32)
    live = lax.broadcasted_iota(jnp.int32, (dests, cap), 1) < counts
    code = jnp.where(live, cells_ref[...], dead)
    fixed = [
        jnp.minimum((offsets_ref[i] * STEPS + 0.5).astype(jnp.int32), STEPS - 1) for i in range(3)
    ]
    first = fixed[0] | (fixed[2] << BITS)
    second = fixed[1] | ((fixed[2] >> (32 - BITS)) << BITS)
    codes = code[:, : cap // 2] | (code[:, cap // 2 :] << 16)
    for dest in range(dests):
        words_ref[dest, :, 0:cap] = first[dest : dest + 1]
        words_ref[dest, :, cap : 2 * cap] = second[dest : dest + 1]
        words_ref[dest, :, 2 * cap :] = codes[dest : dest + 1]


def packed_slots(cells, offsets, counts, width_x, width_y, depth_z):
    dests, cap = cells.shape
    return pl.pallas_call(
        functools.partial(pack_kernel, 2 * width_x * width_y * depth_z),
        out_shape=jax.ShapeDtypeStruct((dests, 1, 5 * cap // 2), jnp.int32),
        in_specs=[pl.BlockSpec(memory_space=pltpu.HBM)] * 3,
        out_specs=pl.BlockSpec(memory_space=pltpu.VMEM),
        scratch_shapes=[
            pltpu.VMEM((dests, cap), jnp.int32),
            pltpu.VMEM((3, dests, cap), jnp.float32),
            pltpu.VMEM((1, dests), jnp.int32),
            pltpu.SemaphoreType.DMA((3,)),
        ],
        compiler_params=pltpu.CompilerParams(vmem_limit_bytes=60 * 1024 * 1024),
        name="pack",
    )(cells, offsets.transpose(1, 0, 2), counts)


def deposit_kernel(width_x, width_y, depth_z, cap, words_ref, after_ref, late_ref, out_ref, acc_ref):
    rows = out_ref.shape[0]
    acc_ref[...] = jnp.zeros_like(acc_ref)
    slot_rows = cap // 128
    source_rows = slot_rows * 5 // 2
    group = 16 // slot_rows
    row_id = lax.broadcasted_iota(jnp.int32, (8, 128), 0)
    z_id = lax.broadcasted_iota(jnp.int32, (depth_z, 128), 0).astype(jnp.float32).astype(jnp.bfloat16)
    one, zero = jnp.bfloat16(1.0), jnp.bfloat16(0.0)

    def body(i, carry):
        block = words_ref[pl.ds(pl.multiple_of(i * group * source_rows, 8), group * source_rows), :]

        def gathered(start, length):
            parts = [block[k * source_rows + start : k * source_rows + start + length] for k in range(group)]
            return parts

        first = jnp.concatenate(gathered(0, slot_rows), axis=0)
        second = jnp.concatenate(gathered(slot_rows, slot_rows), axis=0)
        halves = gathered(2 * slot_rows, slot_rows // 2)
        code = jnp.concatenate([part for half in halves for part in (half & 0xFFFF, (half >> 16) & 0xFFFF)], axis=0)
        inv = 1.0 / STEPS
        fixed_z = ((first >> BITS) & ((1 << (32 - BITS)) - 1)) | ((second >> BITS) << (32 - BITS))
        frac_x = (first & (STEPS - 1)).astype(jnp.float32) * inv
        frac_y = (second & (STEPS - 1)).astype(jnp.float32) * inv
        frac_z = fixed_z.astype(jnp.float32) * inv
        cell_z = (code % depth_z).astype(jnp.float32)
        column = code // depth_z
        cell_y = column % width_y
        cell_x = column // width_y
        past = jnp.where(cell_y == width_y - 1, frac_y, 0.0)
        rest_x, rest_y, rest_z = 1.0 - frac_x, 1.0 - frac_y, 1.0 - frac_z
        weights, hot = [], []
        for k in range(16):
            row = slice(k, k + 1)
            at_y, at_x = cell_y[row], cell_x[row]
            wy = jnp.where(at_y == row_id, rest_y[row], jnp.where(at_y + 1 == row_id, frac_y[row], 0.0))
            wx = jnp.where(at_x == row_id, rest_x[row], jnp.where(at_x + 1 == row_id, frac_x[row], 0.0))
            parts = [wx[x : x + 1] * wy for x in range(width_x + 1)] + [wx * past[row]]
            area = jnp.concatenate(parts, axis=0)
            low, high = area * rest_z[row], area * frac_z[row]
            low_a, high_a = low.astype(jnp.bfloat16), high.astype(jnp.bfloat16)
            low_b = (low - low_a.astype(jnp.float32)).astype(jnp.bfloat16)
            high_b = (high - high_a.astype(jnp.float32)).astype(jnp.bfloat16)
            weights.append(jnp.concatenate([low_a, low_b, high_a, high_b], axis=0))
            at_z = jnp.broadcast_to(cell_z[row], (depth_z, 128)).astype(jnp.bfloat16)
            hot.append(jnp.where(at_z == z_id, one, zero))
        acc_ref[...] += lax.dot_general(
            jnp.concatenate(weights, axis=1),
            jnp.concatenate(hot, axis=1),
            (((1,), (1,)), ((), ())),
            preferred_element_type=jnp.float32,
        )
        return carry

    lax.fori_loop(0, words_ref.shape[0] // (group * source_rows), body, 0, unroll=16)
    low = acc_ref[0:rows] + acc_ref[rows : 2 * rows]
    high = acc_ref[2 * rows : 3 * rows] + acc_ref[3 * rows : 4 * rows]
    out_ref[...] = low + pltpu.roll(high, 1, axis=1)


def deposit(words, after, late, cap, width_x, width_y, depth_z):
    rows = (width_x + 1) * width_y + 8
    return pl.pallas_call(
        functools.partial(deposit_kernel, width_x, width_y, depth_z, cap),
        out_shape=jax.ShapeDtypeStruct((rows, depth_z), jnp.float32),
        in_specs=[pl.BlockSpec(memory_space=pltpu.VMEM)] * 3,
        out_specs=pl.BlockSpec(memory_space=pltpu.VMEM),
        scratch_shapes=[pltpu.VMEM((4 * rows, depth_z), jnp.float32)],
        compiler_params=pltpu.CompilerParams(vmem_limit_bytes=16 * 1024 * 1024),
        name="deposit",
    )(words.reshape(-1, 128), after, late)


def combine_kernel(width_x, width_y, own_ref, other_ref, near_ref, far_ref):
    full_y = 2 * width_y
    spill = (width_x + 1) * width_y
    top = lax.broadcasted_iota(jnp.int32, (width_y, own_ref.shape[1]), 0) == 0
    planes = []
    for x in range(width_x + 1):
        rows, edge = slice(x * width_y, (x + 1) * width_y), slice(spill + x, spill + x + 1)
        upper = own_ref[rows] + jnp.where(top, other_ref[edge], 0.0)
        lower = other_ref[rows] + jnp.where(top, own_ref[edge], 0.0)
        near_ref[x * full_y : x * full_y + width_y] = upper
        near_ref[x * full_y + width_y : (x + 1) * full_y] = lower
        planes.append((upper, lower))
    upward = lax.axis_index("sub") == 0
    for i, (up, down) in enumerate(((width_x - 1, 0), (width_x, 0))):
        for half in range(2):
            start = i * full_y + half * width_y
            far_ref[start : start + width_y] = jnp.where(upward, planes[up][half], planes[down][half])


def combined(own, other, width_x, width_y):
    depth_z = own.shape[1]
    full_y = 2 * width_y
    return pl.pallas_call(
        functools.partial(combine_kernel, width_x, width_y),
        out_shape=(
            jax.ShapeDtypeStruct(((width_x + 1) * full_y, depth_z), jnp.float32),
            jax.ShapeDtypeStruct((2 * full_y, depth_z), jnp.float32),
        ),
        in_specs=[pl.BlockSpec(memory_space=pltpu.VMEM)] * 2,
        out_specs=(pl.BlockSpec(memory_space=pltpu.VMEM),) * 2,
        compiler_params=pltpu.CompilerParams(vmem_limit_bytes=4 * 1024 * 1024),
        name="combine",
    )(own, other)


CH = 16
RIM = 16


def dot(a, b, dims=((1,), (0,))):
    return lax.dot_general(a, b, (dims, ((), ())), preferred_element_type=jnp.float32)


def iota(shape, axis):
    return lax.broadcasted_iota(jnp.int32, shape, axis)


def weights_kernel(
    full_y, raw_ref, after_ref, mats_ref, wfirst_ref, whead_ref, square, taps_ref
):
    lanes = full_y * CH
    f32, bf16 = jnp.float32, jnp.bfloat16
    slot = iota((CH, 128), 1) // CH

    def turned(x, by):
        return x if by % 128 == 0 else pltpu.roll(x, by % 128, axis=1)

    square[...] = jnp.zeros_like(square)
    for which in range(2):
        square[0:CH, :] = raw_ref[:, which * 512 : (which + 1) * 512].astype(f32)
        flipped = jnp.transpose(square[...])
        for dx in range(3):
            for dz in range(3):
                ahead = back = jnp.zeros((CH, 128), f32)
                for dy in range(3):
                    start = (dx * 9 + dy * 3 + dz) * CH
                    ahead = ahead + turned(flipped[start : start + CH], dy * CH)
                    block = start // 128 * 128
                    picked = jnp.where(slot == (start - block) // CH, square[0:CH, block : block + 128], 0.0)
                    back = back + turned(picked, dy * CH - (start - block))
                rows = slice((dx * 3 + dz) * CH, (dx * 3 + dz + 1) * CH)
                taps_ref[which, rows, :] = ahead.astype(bf16)
                taps_ref[2 + which, rows, :] = back.astype(bf16)

    row, lane = iota((128, lanes), 0), iota((128, lanes), 1)
    same = row % CH == lane % CH
    shift, lane_y = row // CH - 1, lane // CH

    def body(y, carry):
        forward = jnp.where(same & (lane_y == (y - shift + full_y) % full_y), 1.0, 0.0).astype(bf16)
        back = jnp.where(same & (lane_y == (y + shift + full_y) % full_y), 1.0, 0.0).astype(bf16)
        for which in range(4):
            spread = dot(taps_ref[which], forward if which < 2 else back).astype(bf16)
            for dx in range(3):
                for dz in range(3):
                    tap = dx * 3 + dz if which < 2 else (2 - dx) * 3 + 2 - dz
                    start = pl.multiple_of(dz * lanes + y * CH, CH)
                    mats_ref[which, dx, pl.ds(start, CH), :] = spread[tap * CH : (tap + 1) * CH]
        return carry

    lax.fori_loop(0, full_y, body, 0, unroll=4)

    rows = 9 * full_y
    at_y, at_lane = iota((rows, lanes), 0) % full_y, iota((rows, lanes), 1) // CH
    square[...] = jnp.zeros_like(square)
    square[0:CH, 0:128] = raw_ref[:, 1024:1152].astype(f32)
    flipped = jnp.transpose(square[:, 0:128])
    spread_rows = []
    for dx in range(3):
        for dz in range(3):
            line = jnp.zeros((1, 128), f32)
            for dy in range(3):
                tap = dx * 9 + dy * 3 + dz
                line = line + turned(flipped[tap : tap + 1], dy * CH)
            spread_rows.append(jnp.broadcast_to(line, (full_y, 128)))
    first = jnp.concatenate(spread_rows, axis=0).astype(bf16)
    total = jnp.zeros((rows, lanes), f32)
    for dy in range(3):
        pick = jnp.where(same & (row // CH == dy), 1.0, 0.0).astype(bf16)
        total = jnp.where(at_y == (at_lane + dy - 1 + full_y) % full_y, dot(first, pick), total)
    wfirst_ref[...] = total.astype(bf16)

    rows = 3 * full_y
    at_y, at_lane = iota((rows, lanes), 0) % full_y, iota((rows, lanes), 1) // CH
    square[...] = jnp.zeros_like(square)
    square[0:CH, 0:128] = raw_ref[:, 1152:1280].astype(f32)
    head = [jnp.broadcast_to(square[k : k + 1, 0:128], (full_y, 128)) for k in range(3)]
    head = jnp.concatenate(head, axis=0).astype(bf16)
    for half in range(2):
        pick = jnp.where(row == lane % CH + half * CH, 1.0, 0.0).astype(bf16)
        whead_ref[half] = jnp.where(at_y == at_lane, dot(head, pick), 0.0).astype(bf16)


def side_by_side(w_first, w_mid, w_last, w_head):
    def widened(w, columns):
        return jnp.pad(w, ((0, CH - w.shape[0]), (0, columns - w.shape[1])))

    return jnp.concatenate([widened(w_mid, 512), widened(w_last, 512), widened(w_first, 128), widened(w_head, 128)], axis=1)


def weight_matrices(raw, after, full_y):
    lanes = full_y * CH
    return pl.pallas_call(
        functools.partial(weights_kernel, full_y),
        out_shape=(
            jax.ShapeDtypeStruct((4, 3, 3 * lanes, lanes), jnp.bfloat16),
            jax.ShapeDtypeStruct((9 * full_y, lanes), jnp.bfloat16),
            jax.ShapeDtypeStruct((2, 3 * full_y, lanes), jnp.bfloat16),
        ),
        in_specs=[pl.BlockSpec(memory_space=pltpu.VMEM)] * 2,
        out_specs=(pl.BlockSpec(memory_space=pltpu.VMEM),) * 3,
        scratch_shapes=[pltpu.VMEM((128, 512), jnp.float32), pltpu.VMEM((4, 9 * CH, 128), jnp.bfloat16)],
        compiler_params=pltpu.CompilerParams(vmem_limit_bytes=16 * 1024 * 1024),
        cost_estimate=pl.CostEstimate(flops=2 * 4 * 9 * CH * 128 * lanes * full_y, bytes_accessed=8 << 20, transcendentals=0),
        name="weights",
    )(raw, after)


def edges_kernel(width_x, width_y, own_ref, other_ref, middle_ref, edge_ref):
    full_y = 2 * width_y
    upward = lax.axis_index("sub") == 0
    for k in range(3):
        rows = slice(k * full_y, (k + 1) * full_y)
        planes = []
        for x in range(width_x):
            both = [own_ref[k, x].astype(jnp.float32), other_ref[k, x].astype(jnp.float32)]
            planes.append(jnp.concatenate(both, axis=0))
            middle_ref[x, rows] = planes[x].astype(jnp.bfloat16)
        for i in range(2):
            edge_ref[i, rows] = jnp.where(upward, planes[width_x - 2 + i], planes[i]).astype(jnp.bfloat16)


def edges(own, other):
    _, width_x, width_y, depth_z = own.shape
    return pl.pallas_call(
        functools.partial(edges_kernel, width_x, width_y),
        out_shape=(
            jax.ShapeDtypeStruct((width_x, 6 * width_y, depth_z), jnp.bfloat16),
            jax.ShapeDtypeStruct((2, 6 * width_y, depth_z), jnp.bfloat16),
        ),
        in_specs=[pl.BlockSpec(memory_space=pltpu.VMEM)] * 2,
        out_specs=(pl.BlockSpec(memory_space=pltpu.VMEM),) * 2,
        compiler_params=pltpu.CompilerParams(vmem_limit_bytes=4 * 1024 * 1024),
        name="edges",
    )(own, other)


def sigmoid(v):
    return 0.5 + 0.5 * jnp.tanh(0.5 * v)


def chain_kernel(
    width_x,
    width_y,
    near_ref,
    near_mine,
    near_theirs,
    far_mine,
    far_theirs,
    ct_middle,
    ct_mine,
    ct_theirs,
    mats_ref,
    wfirst_ref,
    whead_ref,
    force_mine,
    force_theirs,
    mine_ref,
    theirs_ref,
    ct_ref,
    dens,
    dens_inner,
    one,
    two,
    three,
    g_three,
    g_two,
    pre_one,
    pre_two,
    wg,
):
    full_y = 2 * width_y
    full = ct_middle.shape[2]
    half = full // 2
    depth = half + 2 * RIM
    inner = slice(RIM, RIM + half)
    lanes = full_y * CH
    first_core = lax.axis_index("sub") == 0

    def turned(ref, plane):
        start = plane * full_y
        return jnp.concatenate([ref[start + width_y : start + full_y], ref[start : start + width_y]], axis=0)

    def straight(ref, plane):
        return ref[plane * full_y : (plane + 1) * full_y]

    planes = [straight(near_ref, x) for x in range(width_x + 1)]
    below = [jnp.where(first_core, straight(near_mine, x), turned(near_theirs, x)) for x in range(width_x + 1)]
    above = [jnp.where(first_core, turned(near_theirs, x), straight(near_mine, x)) for x in range(width_x + 1)]
    tail = [jnp.where(first_core, straight(far_mine, x), turned(far_theirs, x)) for x in range(2)]
    ahead = jnp.where(first_core, turned(far_theirs, 0), straight(far_mine, 0))
    column = [tail[0], tail[1] + below[0], *below[1:width_x], below[width_x] + planes[0], *planes[1:width_x]]
    column = column + [planes[width_x] + above[0], *above[1:width_x], above[width_x] + ahead]
    n_dens = 3 * width_x + 2
    def framed(field):
        return jnp.where(first_core, pltpu.roll(field, RIM, axis=1), pltpu.roll(field, half + RIM, axis=1))

    def around(plane):
        return jnp.concatenate([pltpu.roll(plane, 1, axis=1), plane, pltpu.roll(plane, full - 1, axis=1)], axis=0)

    def chosen(field):
        return jnp.where(first_core, field[:, 0:half], field[:, half:full])

    for j in range(n_dens):
        rows = slice(3 * full_y * j, 3 * full_y * (j + 1))
        dens[rows] = around(framed(column[j]))[:, 0:depth].astype(jnp.bfloat16)
        if 0 <= j - 4 < width_x + 2:
            rows = slice(3 * full_y * (j - 4), 3 * full_y * (j - 3))
            dens_inner[rows] = chosen(around(column[j])).astype(jnp.bfloat16)

    ct_inner = []
    for x in range(width_x):
        plane = ct_middle[x].astype(jnp.float32)
        ct_ref[x + 2] = framed(plane)[:, 0:depth].astype(jnp.bfloat16)
        ct_inner.append(chosen(plane).astype(jnp.bfloat16))
    for x in range(2):
        mine, theirs = framed(ct_mine[x].astype(jnp.float32)), framed(ct_theirs[x].astype(jnp.float32))
        halves = [theirs[i * width_y : (i + 1) * width_y] for i in (1, 0, 3, 2, 5, 4)]
        theirs = jnp.concatenate(halves, axis=0)
        ct_ref[x] = jnp.where(first_core, mine, theirs)[:, 0:depth].astype(jnp.bfloat16)
        ct_ref[x + 2 + width_x] = jnp.where(first_core, theirs, mine)[:, 0:depth].astype(jnp.bfloat16)

    def window(x):
        return dens[pl.ds(pl.multiple_of(3 * full_y * x, 3 * full_y), 9 * full_y), :]

    def put(ref, x, field):
        ref[x, :, 0:lanes] = pltpu.roll(field, 1, axis=0).astype(jnp.bfloat16)
        ref[x, :, lanes : 2 * lanes] = field.astype(jnp.bfloat16)
        ref[x, :, 2 * lanes : 3 * lanes] = pltpu.roll(field, depth - 1, axis=0).astype(jnp.bfloat16)

    def conv(ref, x, which):
        total = None
        for dx in range(3):
            part = dot(ref[x + dx : x + dx + 2].reshape(2 * depth, 3 * lanes), mats_ref[which, dx])
            total = part if total is None else total + part
        return total.reshape(2, depth, lanes)

    def slope(v):
        s = sigmoid(v)
        return s * (1.0 + v * (1.0 - s))

    def first_plane(x):
        v = dot(window(x), wfirst_ref[...], ((0,), (0,)))
        if 0 <= x - 4 < width_x:
            pre_one[x - 4] = v
        put(one, x, v * sigmoid(v))

    def second_done(i, both):
        for k in range(2):
            v, x = both[k], 2 * i + k
            if 0 <= x - 2 < width_x + 2:
                pre_two[x - 2] = v
            put(two, x, v * sigmoid(v))

    def third_done(i, both):
        for k in range(2):
            v, x = both[k], 2 * i + k
            s = sigmoid(v)
            if 0 <= x - 2 < width_x:
                three[x - 2] = (v * s).astype(jnp.bfloat16)
            back = dot(ct_ref[x], whead_ref[0], ((0,), (0,)))
            put(g_three, x, back * (s * (1.0 + v * (1.0 - s))))

    def back_done(i, both):
        for k in range(2):
            x = 2 * i + k
            put(g_two, x, both[k] * slope(pre_two[x]))

    layers = ((one, 0, second_done), (two, 1, third_done), (g_three, 3, back_done))
    pairs = [(n_dens - 4 - 2 * layer) // 2 for layer in range(3)]
    order = sorted(
        ((i + 2.6 * layer, layer, i) for layer in range(3) for i in range(pairs[layer])),
    )
    firsts_done = 0
    waiting = None
    for _, layer, i in order:
        if layer == 0:
            while firsts_done < 2 * i + 4:
                first_plane(firsts_done)
                firsts_done += 1
        elif waiting is not None and waiting[0] == layer - 1 and waiting[1] <= i + 1:
            layers[waiting[0]][2](waiting[1], waiting[2])
            waiting = None
        ref, which, done = layers[layer]
        both = conv(ref, 2 * i, which)
        if waiting is not None:
            layers[waiting[0]][2](waiting[1], waiting[2])
        waiting = (layer, i, both)
    layers[waiting[0]][2](waiting[1], waiting[2])

    ct_own = jnp.concatenate(ct_inner, axis=1)
    heads = [
        dot(ct_own, three[:, inner, :].reshape(width_x * half, lanes)),
        dot(ct_own, one[4 : 4 + width_x, inner, lanes : 2 * lanes].reshape(width_x * half, lanes)),
    ]
    for x in range(width_x):
        rows = dot(three[x, inner, :], whead_ref[0], ((1,), (1,)))
        rows = jnp.transpose(rows + dot(one[x + 4, inner, lanes : 2 * lanes], whead_ref[1], ((1,), (1,))))
        for k in range(3):
            start = k * full_y
            force_mine[k, x] = rows[start : start + width_y].astype(jnp.bfloat16)
            force_theirs[k, x] = rows[start + width_y : start + full_y].astype(jnp.bfloat16)

    for which, grads, fields, shift in ((0, g_three, two, (2, 2)), (1, g_two, one, (1, 3))):
        across = [jnp.transpose(grads[x + shift[0], inner, lanes : 2 * lanes]) for x in range(width_x)]
        across = jnp.concatenate(across, axis=1)
        for dx in range(3):
            field = fields[shift[1] + dx : shift[1] + dx + width_x, inner, :]
            wg[which, dx] = dot(across, field.reshape(width_x * half, 3 * lanes))
    grad_one = []
    for i in range(width_x // 2):
        both = conv(g_two, 2 * i, 2)
        for k in range(2):
            x = 2 * i + k
            back = both[k] + dot(ct_ref[x + 2], whead_ref[1], ((0,), (0,)))
            grad_one.append((back * slope(pre_one[x])).astype(jnp.bfloat16)[inner])
    windows = jnp.concatenate(
        [dens_inner[3 * full_y * x : 3 * full_y * (x + 3)] for x in range(width_x)], axis=1
    )
    firsts = dot(windows, jnp.concatenate(grad_one, axis=0))

    lane = iota((CH, 128), 1)

    def gathered(which):
        blocks = [jnp.zeros((CH, 128), jnp.float32) for _ in range(4)]
        for dx in range(3):
            for dz in range(3):
                lined = jnp.zeros((CH, lanes), jnp.float32)
                for y in range(full_y):
                    piece = wg[which, dx, y * CH : (y + 1) * CH, dz * lanes : (dz + 1) * lanes]
                    turn = (lanes - CH * (y - 1)) % lanes
                    lined = lined + (piece if turn == 0 else pltpu.roll(piece, turn, axis=1))
                for dy in range(3):
                    target = (dx * 9 + dy * 3 + dz) * CH
                    turn = (target - dy * CH) % 128
                    piece = jnp.where(lane // CH == dy, lined[:, 0:128], 0.0)
                    blocks[target // 128] += piece if turn == 0 else pltpu.roll(piece, turn, axis=1)
        return blocks

    def folded(rows):
        rows = sum(rows[:, i * 128 : (i + 1) * 128] for i in range(lanes // 128))
        for turn in (64, 32, 16):
            rows = rows + pltpu.roll(rows, turn, axis=1)
        return rows

    last, mid = gathered(0), gathered(1)
    at_y, at_lane = iota((full_y, lanes), 0), iota((full_y, lanes), 1) // CH
    first_rows = []
    for dx in range(3):
        for dy in range(3):
            match = at_y == (at_lane + dy - 1 + full_y) % full_y
            for dz in range(3):
                tap = (dx * 3 + dz) * full_y
                part = jnp.where(match, firsts[tap : tap + full_y, :], 0.0)
                first_rows.append(jnp.sum(part, axis=0, keepdims=True))
    first = folded(jnp.concatenate(first_rows + [jnp.zeros((5, lanes), jnp.float32)], axis=0))
    gap = jnp.zeros((48, 128), jnp.float32)
    last[3] += jnp.transpose(jnp.concatenate([gap, first, gap], axis=0))[0:CH]
    for part_of in range(2):
        rows = []
        for k in range(3):
            part = jnp.where(at_y == at_lane, heads[part_of][k * full_y : (k + 1) * full_y], 0.0)
            rows.append(jnp.sum(part, axis=0, keepdims=True))
        head = folded(jnp.concatenate(rows + [jnp.zeros((CH - 3, lanes), jnp.float32)], axis=0))
        last[3] += jnp.where(lane // CH == 5 + part_of, head, 0.0)
    for block in range(4):
        columns = slice(block * 128, (block + 1) * 128)
        mine_ref[:, columns] = jnp.where(first_core, last[block], mid[block])
        theirs_ref[:, columns] = jnp.where(first_core, mid[block], last[block])


def chain(pieces, mats, wfirst, whead, width_x, width_y, depth_z):
    full_y = 2 * width_y
    lanes = full_y * CH
    half = depth_z // 2
    depth = half + 2 * RIM
    n_dens = 3 * width_x + 2
    bf16, f32 = jnp.bfloat16, jnp.float32
    args = (*pieces, mats, wfirst, whead)
    return pl.pallas_call(
        functools.partial(chain_kernel, width_x, width_y),
        out_shape=(
            jax.ShapeDtypeStruct((3, width_x, width_y, half), bf16),
            jax.ShapeDtypeStruct((3, width_x, width_y, half), bf16),
            jax.ShapeDtypeStruct((CH, 512), f32),
            jax.ShapeDtypeStruct((CH, 512), f32),
        ),
        in_specs=[pl.BlockSpec(memory_space=pltpu.VMEM)] * len(args),
        out_specs=(pl.BlockSpec(memory_space=pltpu.VMEM),) * 4,
        scratch_shapes=[
            pltpu.VMEM((width_x + 4, 3 * full_y, depth), bf16),
            pltpu.VMEM((n_dens * 3 * full_y, depth), bf16),
            pltpu.VMEM(((width_x + 2) * 3 * full_y, half), bf16),
            pltpu.VMEM((n_dens - 2, depth, 3 * lanes), bf16),
            pltpu.VMEM((n_dens - 4, depth, 3 * lanes), bf16),
            pltpu.VMEM((width_x, depth, lanes), bf16),
            pltpu.VMEM((n_dens - 6, depth, 3 * lanes), bf16),
            pltpu.VMEM((n_dens - 8, depth, 3 * lanes), bf16),
            pltpu.VMEM((width_x, depth, lanes), f32),
            pltpu.VMEM((width_x + 2, depth, lanes), f32),
            pltpu.VMEM((2, 3, lanes, 3 * lanes), f32),
        ],
        compiler_params=pltpu.CompilerParams(vmem_limit_bytes=36 * 1024 * 1024),
        name="chain",
    )(*args)


def passed_along(x, axis, by):
    devices = lax.axis_size(axis)
    return lax.ppermute(x, axis, [(i, (i + by) % devices) for i in range(devices)])


def exchanged(x, axis, mask):
    return lax.ppermute(x, axis, [(i, i ^ mask) for i in range(lax.axis_size(axis))])


def summed(mine, theirs, beside):
    total = mine + exchanged(theirs, "sub", 1)
    stride, chips = 1, lax.axis_size("slab")
    while stride < chips:
        if chips // stride >= 4:
            got = [exchanged(total, "slab", stride * i) for i in (1, 2, 3)]
            total = (total + got[0]) + (got[1] + got[2])
            if stride == 1:
                total, beside = lax.optimization_barrier((total, beside))
            stride *= 4
        else:
            total = total + exchanged(total, "slab", stride)
            stride *= 2
    return total, exchanged(total, "sub", 1), beside


def finish_kernel(
    loss_scale, mine_ref, theirs_ref, force_mine, force_theirs, force_ref, first_ref, mid_ref, last_ref, head_ref
):
    first_core = lax.axis_index("sub") == 0
    taps = 27 * CH
    mine, theirs = mine_ref[...] * loss_scale, theirs_ref[...] * loss_scale
    mid = jnp.where(first_core, theirs, mine)
    last = jnp.where(first_core, mine, theirs)
    mid_ref[...] = mid[:, :taps]
    last_ref[...] = last[:, :taps]
    half = force_mine.shape[3]
    for k in range(force_ref.shape[0]):
        for x in range(force_ref.shape[1]):
            ours, other = force_mine[k, x].astype(jnp.float32), force_theirs[k, x].astype(jnp.float32)
            force_ref[k, x, :, 0:half] = jnp.where(first_core, ours, other).astype(jnp.bfloat16)
            force_ref[k, x, :, half:] = jnp.where(first_core, other, ours).astype(jnp.bfloat16)
    both = mine[:, 384:] + theirs[:, 384:]
    first_ref[...] = pltpu.roll(both, 80, axis=1)[:, :27]
    head_ref[...] = pltpu.roll(both, 48, axis=1)[:3, : 2 * CH]


def finished(mine, theirs, force_mine, force_theirs, loss_scale):
    f32 = jnp.float32
    _, width_x, width_y, half = force_mine.shape
    return pl.pallas_call(
        functools.partial(finish_kernel, loss_scale),
        out_shape=(
            jax.ShapeDtypeStruct((3, width_x, width_y, 2 * half), jnp.bfloat16),
            jax.ShapeDtypeStruct((CH, 27), f32),
            jax.ShapeDtypeStruct((CH, 27 * CH), f32),
            jax.ShapeDtypeStruct((CH, 27 * CH), f32),
            jax.ShapeDtypeStruct((3, 2 * CH), f32),
        ),
        in_specs=[pl.BlockSpec(memory_space=pltpu.VMEM)] * 4,
        out_specs=(pl.BlockSpec(memory_space=pltpu.VMEM),) * 5,
        compiler_params=pltpu.CompilerParams(vmem_limit_bytes=4 * 1024 * 1024),
        name="finish",
    )(mine, theirs, force_mine, force_theirs)


def per_device(part_cells, part_offsets, part_counts, w_first, w_mid, w_last, w_head, cotangent):
    n_slab = lax.axis_size("slab")
    n_sub = lax.axis_size("sub")
    axes = ("slab", "sub")
    width_x = cotangent.shape[1]
    width_y = cotangent.shape[2]
    depth_z = cotangent.shape[3]
    cap = part_cells.shape[2]

    def outward(x, by):
        pairs = []
        for i in range(n_slab):
            pairs.append((i * n_sub, (i + by) % n_slab * n_sub))
            pairs.append((i * n_sub + 1, (i - by) % n_slab * n_sub + 1))
        return lax.ppermute(x, axes, pairs)

    raw = side_by_side(w_first, w_mid, w_last, w_head)
    words = packed_slots(part_cells[0], part_offsets[0], part_counts, width_x, width_y, depth_z)
    ct_other = exchanged(cotangent, "sub", 1)
    words, ct_other = lax.optimization_barrier((words, ct_other))
    ct_middle, ct_edge = edges(cotangent, ct_other)
    got = lax.all_to_all(words, axes, split_axis=0, concat_axis=0, tiled=True)
    own = deposit(got, ct_edge, raw, cap, width_x, width_y, depth_z)
    near, far = combined(own, exchanged(own, "sub", 1), width_x, width_y)
    mats, wfirst, whead = weight_matrices(raw, far, n_sub * width_y)
    near_mine, far_mine, ct_mine, whead = lax.optimization_barrier(
        (outward(near, 1), outward(far, 2), outward(ct_edge, 1), whead)
    )
    near_theirs, far_theirs, ct_theirs = (exchanged(piece, "sub", 1) for piece in (near_mine, far_mine, ct_mine))
    pieces = (near, near_mine, near_theirs, far_mine, far_theirs, ct_middle, ct_mine, ct_theirs)
    force_mine, force_theirs, mine, theirs = chain(pieces, mats, wfirst, whead, width_x, width_y, depth_z)
    loss_scale = 1.0 / math.sqrt(width_x * n_slab * width_y * n_sub * depth_z)
    force_theirs = exchanged(force_theirs, "sub", 1)
    mine, theirs, force_theirs = summed(mine, theirs, force_theirs)
    return finished(mine, theirs, force_mine, force_theirs, loss_scale)


def solution(mesh):
    in_specs = (
        P(("slab", "sub"), None, None),
        P(("slab", "sub"), None, None, None),
        P(("slab", "sub"), None),
        P(),
        P(),
        P(),
        P(),
        P(None, "slab", "sub", None),
    )
    out_specs = (P(None, "slab", "sub", None), P(), P(), P(), P())
    return jax.shard_map(
        per_device, mesh=mesh, in_specs=in_specs, out_specs=out_specs, check_vma=False
    )
```
